256 devices in a mesh: sta: 64 (over z, x, y_lo), day: 4 (over y_hi, core).
Axes of the slice: x: 4, y: 4 (y_hi: 2, y_lo: 2; y = y_hi * 2 + y_lo), z: 8, core: 2. Of those that a mesh axis runs over, the one named last changes fastest.
Arguments:
- spectra: bfloat16 [512, 32, 2, 640], P('sta', 'day'), may hold values from -80 to 80
- pairing: int32 [3, 64], replicated, may hold values from 0 to 63, as said below
- station_slot: int32 [512], replicated, may hold values from 0 to 7, as said below
Outputs:
- correlations: bfloat16 [3, 8, 512, 512], P(None, 'day', 'sta')
The draws below stay inside these ranges and needn't reach their ends.
Inputs may be any that keep to these rules, and one draw needn't show every extreme that they name: In every round the table is a perfect matching of the 64 blocks: block b meets pairing[r, b], which meets b back, never b itself; no two blocks meet in two rounds. `station_slot`: within every block of 8 consecutive stations each slot from 0 to 7 appears once.
All inputs are finite; a program needn't handle non-finite values.
Results may differ from the reference program's by a relative error of at most 0.001.
Values may be sent and summed in bfloat16 or wider, within the bound.
A program may use at most 64 MiB of HBM per device.

```python
import math
import jax
import jax.numpy as jnp
from jax import lax

SPB = 8
NFREQ = 640
BIN_LO = 60
SEGLEN = 6000
LAGS = 512
ROUNDS = 3
BLOCKS = 64
STATIONS = 512
SEGS = 32


def draw_spectra(key, part):
    key = jax.random.fold_in(key, 11)
    key_noise, key_station, key_band = jax.random.split(key, 3)
    shape = (STATIONS, SEGS, 2, NFREQ)
    station_scale = jnp.exp(jax.random.uniform(key_station, (STATIONS, 1, 1, 1), jnp.float32, 0.0, math.log(10.0)))
    band_scale = jnp.exp(jax.random.uniform(key_band, (STATIONS, 1, 1, NFREQ), jnp.float32, math.log(0.5), math.log(2.0)))
    noise = jnp.clip(jax.random.normal(key_noise, shape, jnp.float32), -4.0, 4.0)
    return (noise * station_scale * band_scale).astype(jnp.bfloat16)


def draw_pairing(key, part):
    key = jax.random.fold_in(key, 23)
    key_label, key_round = jax.random.split(key)
    labels = jax.random.permutation(key_label, BLOCKS).astype(jnp.int32)
    chosen = jax.random.permutation(key_round, BLOCKS - 1)[:ROUNDS].astype(jnp.int32)
    places = jnp.arange(BLOCKS, dtype=jnp.int32)
    last = BLOCKS - 1

    def matching(turn):
        circle = jnp.mod(2 * turn - places, last)
        partner = jnp.where(places == last, turn, jnp.where(places == turn, last, circle))
        return jnp.zeros((BLOCKS,), jnp.int32).at[labels].set(labels[partner])
    return jax.vmap(matching)(chosen).astype(jnp.int32)


def draw_station_slot(key, part):
    key = jax.random.fold_in(key, 37)
    block_keys = jax.random.split(key, BLOCKS)
    slots = jax.vmap(lambda single: jax.random.permutation(single, SPB))(block_keys)
    return slots.reshape(STATIONS).astype(jnp.int32)


def setup_inputs(seed: int = 0) -> dict:
    streams_of = jax.random.split(jax.random.key(seed), 4)
    spectra = draw_spectra(jax.random.fold_in(streams_of[3], 71), 0)
    pairing = draw_pairing(jax.random.fold_in(streams_of[3], 71), 0)
    station_slot = draw_station_slot(jax.random.fold_in(streams_of[3], 71), 0)
    return {"spectra": spectra, "pairing": pairing, "station_slot": station_slot}


EPS = 1e-06

def lag_table(nfreq, lags):
    bins = BIN_LO + jnp.arange(nfreq, dtype=jnp.int32)
    shifts = jnp.arange(lags, dtype=jnp.int32) - lags // 2
    turns = jnp.mod(bins[:, None] * shifts[None, :], SEGLEN).astype(jnp.float32)
    angle = 2.0 * jnp.pi / SEGLEN * turns
    return jnp.concatenate([jnp.cos(angle), -jnp.sin(angle)], axis=0)

def reference(spectra, pairing, station_slot):
    grouped = spectra.reshape(BLOCKS, SPB, SEGS, 2, NFREQ)
    energy = lax.optimization_barrier(jnp.mean(jnp.square(spectra.astype(jnp.float32)), axis=(1, 2, 3))) + EPS
    energy_blocks = energy.reshape(BLOCKS, SPB)
    slot_order = jnp.argsort(station_slot.reshape(BLOCKS, SPB), axis=1).astype(jnp.int32)
    table = lag_table(NFREQ, LAGS)
    scale = jnp.sqrt(jnp.float32(2 * NFREQ * SEGS))

    def one_round(partner_row):

        def one_block(block):
            partner = partner_row[block]
            own = grouped[block].astype(jnp.float32)
            other = grouped[partner][slot_order[partner]].astype(jnp.float32)
            left = jnp.concatenate([own[:, :, 0], own[:, :, 1]], axis=1)
            right = jnp.stack([jnp.concatenate([other[:, :, 0], other[:, :, 1]], axis=1), jnp.concatenate([-other[:, :, 1], other[:, :, 0]], axis=1)])
            cross = jnp.einsum('isf,cjsf->jicf', left, right, precision=lax.Precision.HIGHEST)
            raw = jnp.dot(cross.reshape(SPB * SPB, 2 * NFREQ), table, precision=lax.Precision.HIGHEST).reshape(SPB, SPB, LAGS)
            energy_j = energy_blocks[partner][slot_order[partner]]
            energy_i = energy_blocks[block]
            result = raw / jnp.sqrt(energy_j[:, None, None] * energy_i[None, :, None]) / scale
            return result.astype(jnp.bfloat16)
        blocks_out = lax.map(one_block, jnp.arange(BLOCKS, dtype=jnp.int32))
        return jnp.transpose(blocks_out, (1, 0, 2, 3)).reshape(SPB, STATIONS, LAGS)
    return jnp.stack([one_round(pairing[index]) for index in range(ROUNDS)])
```

```python
import functools

import jax
import jax.numpy as jnp
import ml_dtypes
import numpy as np
from jax import lax
from jax.experimental import pallas as pl
from jax.experimental.pallas import tpu as pltpu
from jax.sharding import PartitionSpec as P

BIN_LO = 60
SEGLEN = 6000
LAGS = 512
ROUNDS = 3
EPS = 1e-06
NFREQ = 640
SPB = 8
SEG = 8
DAYS = 4
BLOCKS = 64
BANDS = 40
ROWS = 16
LANES = 128
TILES = NFREQ // LANES
LAG_TILES = LAGS // LANES
PARTS = 2 * LAG_TILES + 3
MESH = pl.DeviceIdType.MESH


def lag_table():
    bins = BIN_LO + np.arange(NFREQ, dtype=np.int64)
    shifts = np.arange(LAGS, dtype=np.int64) - LAGS // 2
    turns = np.mod(bins[:, None] * shifts[None, :], SEGLEN)
    angle = 2.0 * np.pi / SEGLEN * turns
    table = np.concatenate([np.cos(angle), -np.sin(angle)], axis=0).astype(np.float32)
    high = table.astype(ml_dtypes.bfloat16)
    low = (table - high.astype(np.float32)).astype(ml_dtypes.bfloat16)
    return np.stack([high, low])


def band_place(band):
    z, turn = band // 5, band % 5
    return z * 8 + (turn + 3 * z) % 8


def kernel(
    x_ref, pairing_ref, slot_ref, table_hbm, out_ref,
    natural, own, sent, banded, picked, returned, partner, cross, sums, met, table,
    table_sem, first_send, first_recv, back_send, back_recv, day_send, day_recv,
):
    sta, day = lax.axis_index("sta"), lax.axis_index("day")
    plane = sta // 8
    turn = (sta % 8 + 5 * plane) % 8
    is_band = turn < 5
    band = plane * 5 + turn

    barrier = pltpu.get_barrier_semaphore()

    def greet(k, carry):
        pl.semaphore_signal(
            barrier, inc=1, device_id=((sta + k) % BLOCKS, day), device_id_type=MESH
        )
        return carry

    lax.fori_loop(1, BLOCKS, greet, 0, unroll=7)
    for k in range(1, DAYS):
        pl.semaphore_signal(
            barrier, inc=1, device_id=(sta, (day + k) % DAYS), device_id_type=MESH
        )
    load_table = pltpu.make_async_copy(table_hbm, table, table_sem)
    load_table.start()

    for c in range(2):
        part = x_ref[:, c, :].astype(jnp.float32)
        natural[c] = part.reshape(SPB, SEG, NFREQ)
    slots = [slot_ref[sta * SPB + i] for i in range(SPB)]
    order = []
    for j in range(SPB):
        at = jnp.int32(0)
        for i in range(1, SPB):
            at = jnp.where(slots[i] == j, i, at)
        order.append(at)
    rows = jnp.concatenate(
        [natural[c, order[j]] for c in range(2) for j in range(SPB)], axis=0
    )
    for t in range(TILES):
        tile = rows[:, t * LANES : (t + 1) * LANES].T.astype(jnp.bfloat16)
        sent[t * 8 : (t + 1) * 8] = tile.reshape(8, ROWS, LANES)

    pl.semaphore_wait(barrier, BLOCKS - 1 + DAYS - 1)

    def first(k):
        to = (sta + k) % BANDS
        place = band_place(to)
        return place, pltpu.make_async_remote_copy(
            src_ref=sent.at[to], dst_ref=banded.at[sta], send_sem=first_send, recv_sem=first_recv,
            device_id=(place, day), device_id_type=MESH,
        )

    def send_first(k, carry):
        place, copy = first(k)

        @pl.when(place != sta)
        def _():
            copy.start()

        return carry

    lax.fori_loop(0, BANDS, send_first, 0, unroll=4)

    @pl.when(is_band)
    def _():
        pltpu.make_async_copy(sent.at[band], banded.at[sta], first_recv).start()

    for seg in range(SEG):
        for c in range(2):
            own[c, seg] = natural[c, :, seg, :]
    own_energy = jnp.zeros((SPB, LANES), jnp.float32)
    for c in range(2):
        for seg in range(SEG):
            square = own[c, seg] * own[c, seg]
            for t in range(TILES):
                own_energy = own_energy + square[:, t * LANES : (t + 1) * LANES]

    @pl.when(is_band)
    def _():
        pltpu.make_async_copy(banded, banded, first_recv).wait()
        for r in range(ROUNDS):

            def pick(b, carry):
                picked[r, b] = banded[pairing_ref[r, b]]
                return carry

            lax.fori_loop(0, BLOCKS, pick, 0, unroll=8)

            def send_back(k, carry):
                to = (sta + k) % BLOCKS
                pltpu.make_async_remote_copy(
                    src_ref=picked.at[r, to], dst_ref=returned.at[r, band],
                    send_sem=back_send, recv_sem=back_recv.at[r],
                    device_id=(to, day), device_id_type=MESH,
                ).start()
                return carry

            pltpu.make_async_copy(
                picked.at[r, sta], returned.at[r, band], back_recv.at[r]
            ).start()
            lax.fori_loop(1, BLOCKS, send_back, 0, unroll=7)

    load_table.wait()
    for r in range(ROUNDS):
        pltpu.make_async_copy(returned.at[r], returned.at[r], back_recv.at[r]).wait()
        for t in range(TILES):
            tile = returned[r, t * 8 : (t + 1) * 8].reshape(LANES, LANES)
            tile = tile.astype(jnp.float32).T
            partner[:, :, :, t * LANES : (t + 1) * LANES] = tile.reshape(2, SPB, SEG, LANES)

        def correlate(j, carry):
            real = jnp.zeros((SPB, NFREQ), jnp.float32)
            imag = jnp.zeros((SPB, NFREQ), jnp.float32)
            for seg in range(SEG):
                x_re, x_im = own[0, seg], own[1, seg]
                y_re = partner[0, j, seg : seg + 1, :]
                y_im = partner[1, j, seg : seg + 1, :]
                real = real + x_re * y_re + x_im * y_im
                imag = imag + x_im * y_re - x_re * y_im
            cross[j, :, :NFREQ] = real
            cross[j, :, NFREQ:] = imag
            return carry

        lax.fori_loop(0, SPB, correlate, 0)
        spectrum = cross[...].reshape(SPB * SPB, 2 * NFREQ)
        high = spectrum.astype(jnp.bfloat16)
        low = (spectrum - high.astype(jnp.float32)).astype(jnp.bfloat16)
        dot = functools.partial(jnp.dot, preferred_element_type=jnp.float32)
        raw = dot(high, table[0]) + dot(low, table[0]) + dot(high, table[1])
        for j in range(SPB):
            to, at = j // 2, j % 2
            for t in range(LAG_TILES):
                sums[r, to, at * LAG_TILES + t] = raw[
                    j * SPB : (j + 1) * SPB, t * LANES : (t + 1) * LANES
                ]
            energy = jnp.zeros((SEG, LANES), jnp.float32)
            for c in range(2):
                for t in range(TILES):
                    y = partner[c, j, :, t * LANES : (t + 1) * LANES]
                    energy = energy + y * y
            sums[r, to, 2 * LAG_TILES + 1 + at] = energy
        for to in range(DAYS):
            sums[r, to, 2 * LAG_TILES] = own_energy
        for k in range(1, DAYS):
            to = (day + k) % DAYS
            pltpu.make_async_remote_copy(
                src_ref=sums.at[r, to], dst_ref=met.at[r, day], send_sem=day_send, recv_sem=day_recv.at[r],
                device_id=(sta, to), device_id_type=MESH,
            ).start()
        pltpu.make_async_copy(sums.at[r, day], met.at[r, day], day_recv.at[r]).start()

    for r in range(ROUNDS):
        pltpu.make_async_copy(met.at[r], met.at[r], day_recv.at[r]).wait()
        total = met[r, 0] + met[r, 1] + met[r, 2] + met[r, 3]
        count = float(SEG * DAYS * 2 * NFREQ)
        energy_i = jnp.sum(total[2 * LAG_TILES], axis=1, keepdims=True) / count + EPS
        for at in range(2):
            energy_j = jnp.sum(total[2 * LAG_TILES + 1 + at], axis=1, keepdims=True)
            energy_j = jnp.sum(energy_j, axis=0, keepdims=True) / count + EPS
            scale = 1.0 / (jnp.sqrt(energy_j * energy_i) * np.float32(np.sqrt(count)))
            for t in range(LAG_TILES):
                out_ref[r, at, :, t * LANES : (t + 1) * LANES] = (
                    total[at * LAG_TILES + t] * scale
                ).astype(jnp.bfloat16)

    @pl.when(is_band)
    def _():
        pltpu.make_async_copy(
            sent.at[pl.ds(0, BANDS - 1)], sent.at[pl.ds(0, BANDS - 1)], first_send
        ).wait()
        for r in range(ROUNDS):
            pltpu.make_async_copy(
                picked.at[r, pl.ds(0, BLOCKS - 1)], picked.at[r, pl.ds(0, BLOCKS - 1)], back_send
            ).wait()

    @pl.when(jnp.logical_not(is_band))
    def _():
        pltpu.make_async_copy(sent, sent, first_send).wait()

    for r in range(ROUNDS):
        pltpu.make_async_copy(
            sums.at[r, pl.ds(0, DAYS - 1)], sums.at[r, pl.ds(0, DAYS - 1)], day_send
        ).wait()


def per_device(spectra, pairing, station_slot):
    x = spectra.reshape(SPB * SEG, 2, NFREQ)
    vmem = pl.BlockSpec(memory_space=pltpu.VMEM)
    smem = pl.BlockSpec(memory_space=pltpu.SMEM)
    dma = pltpu.SemaphoreType.DMA
    f32, bf16 = jnp.float32, jnp.bfloat16
    return pl.pallas_call(
        kernel,
        out_shape=jax.ShapeDtypeStruct((ROUNDS, 2, SPB, LAGS), bf16),
        in_specs=[vmem, smem, smem, pl.BlockSpec(memory_space=pl.ANY)],
        out_specs=vmem,
        scratch_shapes=[
            pltpu.VMEM((2, SPB, SEG, NFREQ), f32),
            pltpu.VMEM((2, SEG, SPB, NFREQ), f32),
            pltpu.VMEM((BANDS, ROWS, LANES), bf16),
            pltpu.VMEM((BLOCKS, ROWS, LANES), bf16),
            pltpu.VMEM((ROUNDS, BLOCKS, ROWS, LANES), bf16),
            pltpu.VMEM((ROUNDS, BANDS, ROWS, LANES), bf16),
            pltpu.VMEM((2, SPB, SEG, NFREQ), f32),
            pltpu.VMEM((SPB, SPB, 2 * NFREQ), f32),
            pltpu.VMEM((ROUNDS, DAYS, PARTS, SPB, LANES), f32),
            pltpu.VMEM((ROUNDS, DAYS, PARTS, SPB, LANES), f32),
            pltpu.VMEM((2, 2 * NFREQ, LAGS), bf16),
            dma, dma, dma, dma, dma((ROUNDS,)), dma, dma((ROUNDS,)),
        ],
        compiler_params=pltpu.CompilerParams(
            collective_id=0, has_side_effects=True, vmem_limit_bytes=48 * 1024 * 1024
        ),
        name="correlate",
    )(x, pairing, station_slot, jnp.asarray(lag_table()))


def solution(mesh):
    in_specs = (P("sta", "day", None, None), P(), P())
    out_specs = P(None, "day", "sta", None)
    return jax.shard_map(
        per_device, mesh=mesh, in_specs=in_specs, out_specs=out_specs, check_vma=False
    )
```

```python
import functools

import jax
import jax.numpy as jnp
import ml_dtypes
import numpy as np
from jax import lax
from jax.experimental import pallas as pl
from jax.experimental.pallas import tpu as pltpu
from jax.sharding import PartitionSpec as P

BIN_LO = 60
SEGLEN = 6000
LAGS = 512
ROUNDS = 3
EPS = 1e-06
NFREQ = 640
SPB = 8
SEG = 8
DAYS = 4
BLOCKS = 64
BANDS = 10
KEPT = BANDS * DAYS
ROWS = 16
LANES = 128
PIECE = 32
TILES = NFREQ // LANES
WHOLE = 512
MESH = pl.DeviceIdType.MESH


def lag_table():
    bins = BIN_LO + np.arange(NFREQ, dtype=np.int64)
    shifts = np.arange(LAGS, dtype=np.int64) - LAGS // 2
    turns = np.mod(bins[:, None] * shifts[None, :], SEGLEN)
    angle = 2.0 * np.pi / SEGLEN * turns
    table = np.concatenate([np.cos(angle), -np.sin(angle)], axis=0).astype(np.float32)
    high = table.astype(ml_dtypes.bfloat16)
    low = (table - high.astype(np.float32)).astype(ml_dtypes.bfloat16)
    return np.stack([high, low])


def keeper(kept, core):
    z, turn = kept // 5, kept % 5
    return z * 8 + (turn + 3 * core + 2 * z) % 8


def kernel(
    x_hbm, pairing_hbm, slot_hbm, table_hbm, out_ref,
    spectra, pairing_ref, slot_ref, natural, own, sent, banded, picked, returned, partner, cross, table,
    load_sem, first_send, first_recv, back_send, back_recv, own_send, own_recv,
):
    sta, day = lax.axis_index("sta"), lax.axis_index("day")
    plane = sta // 8
    turn = (sta % 8 + 6 * plane + 5 * (day % 2)) % 8
    is_keeper = turn < 5
    kept = plane * 5 + turn
    band, origin = kept // DAYS, kept % DAYS
    keeps_own = jnp.logical_and(is_keeper, origin == day)

    loads = [
        pltpu.make_async_copy(source, target, load_sem.at[i])
        for i, (source, target) in enumerate(
            [(x_hbm, spectra.at[day]), (slot_hbm, slot_ref), (pairing_hbm, pairing_ref), (table_hbm, table)]
        )
    ]
    for load in loads:
        load.start()

    barrier = pltpu.get_barrier_semaphore()

    def greet(place, to_day):
        pl.semaphore_signal(barrier, inc=1, device_id=(place, to_day), device_id_type=MESH)

    @pl.when(is_keeper)
    def _():
        def greet_block(k, carry):
            greet((sta + k) % BLOCKS, origin)
            return carry

        lax.fori_loop(1, BLOCKS, greet_block, 0, unroll=7)

        @pl.when(origin != day)
        def _():
            greet(sta, origin)

    def greet_keeper(k, carry):
        place = keeper((sta + k) % KEPT, day % 2)

        @pl.when(place != sta)
        def _():
            greet(place, day)

        return carry

    lax.fori_loop(0, KEPT, greet_keeper, 0, unroll=4)
    for k in range(1, DAYS):
        greet(sta, (day + k) % DAYS)

    for load in loads[:2]:
        load.wait()

    def split(day_from):
        for c in range(2):
            part = spectra[day_from, :, c, :].astype(jnp.float32)
            natural[c] = part.reshape(SPB, SEG, NFREQ)

    split(day)
    slots = [slot_ref[sta * SPB + i] for i in range(SPB)]
    order = []
    for j in range(SPB):
        at = jnp.int32(0)
        for i in range(1, SPB):
            at = jnp.where(slots[i] == j, i, at)
        order.append(at)
    pairs = [
        jnp.concatenate(
            [natural[c, order[2 * to + j]] for c in range(2) for j in range(2)], axis=0
        )
        for to in range(DAYS)
    ]
    quarter = lax.broadcasted_iota(jnp.int32, (PIECE, LANES), 1) // PIECE
    for to in range(DAYS):
        tile = jnp.concatenate(
            [pairs[to][:, g * LANES : (g + 1) * LANES] for g in range(4)], axis=0
        )
        sent[to * BANDS : to * BANDS + 8] = tile.T.astype(jnp.bfloat16).reshape(8, ROWS, LANES)
    rest = []
    for g in range(4):
        piece = jnp.zeros((PIECE, LANES), jnp.float32)
        for to in range(DAYS):
            moved = pairs[to][:, WHOLE:]
            if to != g:
                moved = pltpu.roll(moved, (PIECE * (to - g)) % LANES, 1)
            piece = jnp.where(quarter == to, moved, piece)
        rest.append(piece)
    rest = jnp.concatenate(rest, axis=0).T.astype(jnp.bfloat16)
    for to in range(DAYS):
        sent[to * BANDS + 8 : (to + 1) * BANDS] = rest[to * PIECE : (to + 1) * PIECE].reshape(
            2, ROWS, LANES
        )

    loads[2].wait()
    greetings = KEPT + DAYS - 1 + jnp.where(is_keeper, BLOCKS - 1, 0) - jnp.where(keeps_own, 1, 0)
    pl.semaphore_wait(barrier, greetings)

    def send_first(k, carry):
        at = (sta + k) % KEPT
        to = at // BANDS
        place = keeper(at % BANDS * DAYS + day, to % 2)

        @pl.when(jnp.logical_or(place != sta, to != day))
        def _():
            pltpu.make_async_remote_copy(
                src_ref=sent.at[at], dst_ref=banded.at[sta], send_sem=first_send, recv_sem=first_recv,
                device_id=(place, to), device_id_type=MESH,
            ).start()

        return carry

    lax.fori_loop(0, KEPT, send_first, 0, unroll=4)

    @pl.when(keeps_own)
    def _():
        pltpu.make_async_copy(sent.at[day * BANDS + band], banded.at[sta], first_recv).start()

    for k in range(1, DAYS):
        pltpu.make_async_remote_copy(
            src_ref=spectra.at[day], dst_ref=spectra.at[day], send_sem=own_send, recv_sem=own_recv.at[k - 1],
            device_id=(sta, (day + k) % DAYS), device_id_type=MESH,
        ).start()

    @pl.when(is_keeper)
    def _():
        pltpu.make_async_copy(banded, banded, first_recv).wait()
        for r in range(ROUNDS):

            def pick(b, carry):
                picked[r, b] = banded[pairing_ref[r, b]]
                return carry

            lax.fori_loop(0, BLOCKS, pick, 0, unroll=8)

            def send_back(k, carry):
                to = (sta + k) % BLOCKS
                pltpu.make_async_remote_copy(
                    src_ref=picked.at[r, to], dst_ref=returned.at[r, origin * BANDS + band],
                    send_sem=back_send, recv_sem=back_recv.at[r],
                    device_id=(to, day), device_id_type=MESH,
                ).start()
                return carry

            pltpu.make_async_copy(
                picked.at[r, sta], returned.at[r, origin * BANDS + band], back_recv.at[r]
            ).start()
            lax.fori_loop(1, BLOCKS, send_back, 0, unroll=7)

    for k in range(1, DAYS):
        pltpu.make_async_copy(spectra.at[0], spectra.at[0], own_recv.at[k - 1]).wait()
    square = jnp.zeros((SPB, LANES), jnp.float32)
    for q in range(DAYS):
        split(q)
        for c in range(2):
            for seg in range(SEG):
                x = natural[c, :, seg, :]
                own[c, q, seg] = x
                for t in range(TILES):
                    x_t = x[:, t * LANES : (t + 1) * LANES]
                    square = square + x_t * x_t
    count = float(SEG * DAYS * 2 * NFREQ)
    energy_i = jnp.sum(square, axis=1, keepdims=True) / count + EPS

    loads[3].wait()
    dot = functools.partial(jnp.dot, preferred_element_type=jnp.float32)
    for r in range(ROUNDS):
        pltpu.make_async_copy(returned.at[r], returned.at[r], back_recv.at[r]).wait()
        for q in range(DAYS):
            tile = returned[r, q * BANDS : q * BANDS + 8].reshape(LANES, LANES)
            tile = tile.astype(jnp.float32).T.reshape(4, 2, 2, SEG, LANES)
            for g in range(4):
                partner[:, :, q, :, g * LANES : (g + 1) * LANES] = tile[g]
        rest = jnp.concatenate(
            [
                returned[r, q * BANDS + 8 : (q + 1) * BANDS].reshape(PIECE, LANES)
                for q in range(DAYS)
            ],
            axis=0,
        )
        rest = rest.astype(jnp.float32).T
        for q in range(DAYS):
            piece = jnp.zeros((PIECE, LANES), jnp.float32)
            for g in range(4):
                moved = rest[g * PIECE : (g + 1) * PIECE]
                if g != q:
                    moved = pltpu.roll(moved, (PIECE * (g - q)) % LANES, 1)
                piece = jnp.where(quarter == g, moved, piece)
            partner[:, :, q, :, WHOLE:] = piece.reshape(2, 2, SEG, LANES)

        def correlate(q, sums):
            sums = list(sums)
            for seg in range(SEG):
                x_re, x_im = own[0, q, seg], own[1, q, seg]
                for j in range(2):
                    y_re = partner[0, j, q, seg : seg + 1, :]
                    y_im = partner[1, j, q, seg : seg + 1, :]
                    sums[2 * j] = sums[2 * j] + x_re * y_re + x_im * y_im
                    sums[2 * j + 1] = sums[2 * j + 1] + x_im * y_re - x_re * y_im
            return tuple(sums)

        zero = jnp.zeros((SPB, NFREQ), jnp.float32)
        sums = lax.fori_loop(0, DAYS, correlate, (zero,) * 4)
        for j in range(2):
            for c in range(2):
                cross[j * SPB : (j + 1) * SPB, c * NFREQ : (c + 1) * NFREQ] = sums[2 * j + c]
        spectrum = cross[...]
        high = spectrum.astype(jnp.bfloat16)
        low = (spectrum - high.astype(jnp.float32)).astype(jnp.bfloat16)
        raw = dot(high, table[0]) + dot(low, table[0]) + dot(high, table[1])
        for j in range(2):
            square = jnp.zeros((SEG, LANES), jnp.float32)
            for c in range(2):
                for q in range(DAYS):
                    for t in range(TILES):
                        y = partner[c, j, q, :, t * LANES : (t + 1) * LANES]
                        square = square + y * y
            energy_j = jnp.sum(square, axis=1, keepdims=True)
            energy_j = jnp.sum(energy_j, axis=0, keepdims=True) / count + EPS
            scale = 1.0 / (jnp.sqrt(energy_j * energy_i) * np.float32(np.sqrt(count)))
            out_ref[r, j] = (raw[j * SPB : (j + 1) * SPB] * scale).astype(jnp.bfloat16)

    @pl.when(keeps_own)
    def _():
        rest_sent = sent.at[pl.ds(0, KEPT - 1)]
        pltpu.make_async_copy(rest_sent, rest_sent, first_send).wait()

    @pl.when(jnp.logical_not(keeps_own))
    def _():
        pltpu.make_async_copy(sent, sent, first_send).wait()

    @pl.when(is_keeper)
    def _():
        for r in range(ROUNDS):
            rest_sent = picked.at[r, pl.ds(0, BLOCKS - 1)]
            pltpu.make_async_copy(rest_sent, rest_sent, back_send).wait()

    rest_sent = spectra.at[pl.ds(0, DAYS - 1)]
    pltpu.make_async_copy(rest_sent, rest_sent, own_send).wait()


def per_device(spectra, pairing, station_slot):
    x = spectra.reshape(SPB * SEG, 2, NFREQ)
    hbm = pl.BlockSpec(memory_space=pltpu.HBM)
    dma = pltpu.SemaphoreType.DMA
    f32, bf16 = jnp.float32, jnp.bfloat16
    return pl.pallas_call(
        kernel,
        out_shape=jax.ShapeDtypeStruct((ROUNDS, 2, SPB, LAGS), bf16),
        in_specs=[hbm] * 4,
        out_specs=pl.BlockSpec(memory_space=pltpu.VMEM),
        scratch_shapes=[
            pltpu.VMEM((DAYS,) + x.shape, bf16),
            pltpu.SMEM(pairing.shape, jnp.int32),
            pltpu.SMEM(station_slot.shape, jnp.int32),
            pltpu.VMEM((2, SPB, SEG, NFREQ), f32),
            pltpu.VMEM((2, DAYS, SEG, SPB, NFREQ), f32),
            pltpu.VMEM((KEPT, ROWS, LANES), bf16),
            pltpu.VMEM((BLOCKS, ROWS, LANES), bf16),
            pltpu.VMEM((ROUNDS, BLOCKS, ROWS, LANES), bf16),
            pltpu.VMEM((ROUNDS, KEPT, ROWS, LANES), bf16),
            pltpu.VMEM((2, 2, DAYS, SEG, NFREQ), f32),
            pltpu.VMEM((2 * SPB, 2 * NFREQ), f32),
            pltpu.VMEM((2, 2 * NFREQ, LAGS), bf16),
            dma((4,)), dma, dma, dma, dma((ROUNDS,)), dma, dma((DAYS - 1,)),
        ],
        compiler_params=pltpu.CompilerParams(
            collective_id=0, has_side_effects=True, vmem_limit_bytes=63 * 1024 * 1024
        ),
        name="correlate",
    )(x, pairing, station_slot, jnp.asarray(lag_table()))


def solution(mesh):
    in_specs = (P("sta", "day", None, None), P(), P())
    out_specs = P(None, "day", "sta", None)
    return jax.shard_map(
        per_device, mesh=mesh, in_specs=in_specs, out_specs=out_specs, check_vma=False
    )
```

```python
import functools

import jax
import jax.numpy as jnp
import ml_dtypes
import numpy as np
from jax import lax
from jax.experimental import pallas as pl
from jax.experimental.pallas import tpu as pltpu
from jax.sharding import PartitionSpec as P

BIN_LO = 60
SEGLEN = 6000
LAGS = 512
ROUNDS = 3
EPS = 1e-06
NFREQ = 640
SPB = 8
SEG = 8
DAYS = 4
BLOCKS = 64
BANDS = 10
KEPT = BANDS * DAYS
ROWS = 16
LANES = 128
PIECE = 32
TILES = NFREQ // LANES
WHOLE = 512
MESH = pl.DeviceIdType.MESH


def lag_table():
    bins = BIN_LO + np.arange(NFREQ, dtype=np.int64)
    shifts = np.arange(LAGS, dtype=np.int64) - LAGS // 2
    turns = np.mod(bins[:, None] * shifts[None, :], SEGLEN)
    angle = 2.0 * np.pi / SEGLEN * turns
    table = np.concatenate([np.cos(angle), -np.sin(angle)], axis=0).astype(np.float32)
    high = table.astype(ml_dtypes.bfloat16)
    low = (table - high.astype(np.float32)).astype(ml_dtypes.bfloat16)
    return np.stack([high, low])


def keeper(kept, core):
    z, turn = kept // 5, kept % 5
    return z * 8 + (turn + 3 * core + 2 * z) % 8


def outward(k, half):
    return half + (k + 1) // 2 * (1 - 2 * (k % 2))


def far_first(sta, k):
    plane = (sta // 8 + outward(k // 8, 4)) % 8
    return plane * 8 + (sta % 8 + k % 8 + 1) % 8


def kernel(
    x_hbm, pairing_hbm, slot_hbm, table_hbm, out_ref,
    spectra, pairing_ref, slot_ref, natural, own, sent, banded, picked, returned, partner, cross, table,
    load_sem, first_send, first_recv, back_send, back_recv, own_send, own_recv,
):
    sta, day = lax.axis_index("sta"), lax.axis_index("day")
    plane = sta // 8
    turn = (sta % 8 + 6 * plane + 5 * (day % 2)) % 8
    is_keeper = turn < 5
    kept = plane * 5 + turn
    band, origin = kept // DAYS, kept % DAYS
    keeps_own = jnp.logical_and(is_keeper, origin == day)

    barrier = pltpu.get_barrier_semaphore()

    def greet(place, to_day):
        pl.semaphore_signal(barrier, inc=1, device_id=(place, to_day), device_id_type=MESH)

    @pl.when(is_keeper)
    def _():
        def greet_block(k, carry):
            greet(far_first(sta, k), origin)
            return carry

        lax.fori_loop(0, BLOCKS - 1, greet_block, 0, unroll=7)

        @pl.when(origin != day)
        def _():
            greet(sta, origin)

    for k in range(1, DAYS):
        greet(sta, (day + k) % DAYS)

    loads = [
        pltpu.make_async_copy(source, target, load_sem.at[i])
        for i, (source, target) in enumerate(
            [(x_hbm, spectra.at[day]), (slot_hbm, slot_ref), (pairing_hbm, pairing_ref), (table_hbm, table)]
        )
    ]
    for load in loads:
        load.start()

    for load in loads[:2]:
        load.wait()

    def split(day_from):
        for c in range(2):
            part = spectra[day_from, :, c, :].astype(jnp.float32)
            natural[c] = part.reshape(SPB, SEG, NFREQ)

    split(day)
    slots = [slot_ref[sta * SPB + i] for i in range(SPB)]
    order = []
    for j in range(SPB):
        at = jnp.int32(0)
        for i in range(1, SPB):
            at = jnp.where(slots[i] == j, i, at)
        order.append(at)
    pairs = [
        jnp.concatenate(
            [natural[c, order[2 * to + j]] for c in range(2) for j in range(2)], axis=0
        )
        for to in range(DAYS)
    ]
    quarter = lax.broadcasted_iota(jnp.int32, (PIECE, LANES), 1) // PIECE
    for to in range(DAYS):
        tile = jnp.concatenate(
            [pairs[to][:, g * LANES : (g + 1) * LANES] for g in range(4)], axis=0
        )
        sent[to * BANDS : to * BANDS + 8] = tile.T.astype(jnp.bfloat16).reshape(8, ROWS, LANES)
    rest = []
    for g in range(4):
        piece = jnp.zeros((PIECE, LANES), jnp.float32)
        for to in range(DAYS):
            moved = pairs[to][:, WHOLE:]
            if to != g:
                moved = pltpu.roll(moved, (PIECE * (to - g)) % LANES, 1)
            piece = jnp.where(quarter == to, moved, piece)
        rest.append(piece)
    rest = jnp.concatenate(rest, axis=0).T.astype(jnp.bfloat16)
    for to in range(DAYS):
        sent[to * BANDS + 8 : (to + 1) * BANDS] = rest[to * PIECE : (to + 1) * PIECE].reshape(
            2, ROWS, LANES
        )

    loads[2].wait()
    greetings = KEPT + DAYS - 1 - jnp.where(keeps_own, 1, 0)
    pl.semaphore_wait(barrier, greetings)

    def send_first(k, carry):
        to = (sta + k) % DAYS
        to_band = (plane * BANDS // 8 + outward(k // DAYS, BANDS // 2)) % BANDS
        at = to * BANDS + to_band
        place = keeper(to_band * DAYS + day, to % 2)

        @pl.when(jnp.logical_or(place != sta, to != day))
        def _():
            pltpu.make_async_remote_copy(
                src_ref=sent.at[at], dst_ref=banded.at[sta], send_sem=first_send, recv_sem=first_recv,
                device_id=(place, to), device_id_type=MESH,
            ).start()

        return carry

    lax.fori_loop(0, KEPT, send_first, 0, unroll=4)

    @pl.when(keeps_own)
    def _():
        pltpu.make_async_copy(sent.at[day * BANDS + band], banded.at[sta], first_recv).start()

    for k in range(1, DAYS):
        pltpu.make_async_remote_copy(
            src_ref=spectra.at[day], dst_ref=spectra.at[day], send_sem=own_send, recv_sem=own_recv.at[k - 1],
            device_id=(sta, (day + k) % DAYS), device_id_type=MESH,
        ).start()

    @pl.when(is_keeper)
    def _():
        pltpu.make_async_copy(banded, banded, first_recv).wait()
        for r in range(ROUNDS):

            def pick(b, carry):
                picked[r, b] = banded[pairing_ref[r, b]]
                return carry

            lax.fori_loop(0, BLOCKS, pick, 0, unroll=8)

            def send_back(k, carry):
                to = far_first(sta, k)
                pltpu.make_async_remote_copy(
                    src_ref=picked.at[r, to], dst_ref=returned.at[r, origin * BANDS + band],
                    send_sem=back_send, recv_sem=back_recv.at[r],
                    device_id=(to, day), device_id_type=MESH,
                ).start()
                return carry

            pltpu.make_async_copy(
                picked.at[r, sta], returned.at[r, origin * BANDS + band], back_recv.at[r]
            ).start()
            lax.fori_loop(0, BLOCKS - 1, send_back, 0, unroll=7)

    for k in range(1, DAYS):
        pltpu.make_async_copy(spectra.at[0], spectra.at[0], own_recv.at[k - 1]).wait()
    square = jnp.zeros((SPB, LANES), jnp.float32)
    for q in range(DAYS):
        split(q)
        for c in range(2):
            for seg in range(SEG):
                x = natural[c, :, seg, :]
                own[c, q, seg] = x
                for t in range(TILES):
                    x_t = x[:, t * LANES : (t + 1) * LANES]
                    square = square + x_t * x_t
    count = float(SEG * DAYS * 2 * NFREQ)
    energy_i = jnp.sum(square, axis=1, keepdims=True) / count + EPS

    loads[3].wait()
    dot = functools.partial(jnp.dot, preferred_element_type=jnp.float32)
    for r in range(ROUNDS):
        pltpu.make_async_copy(returned.at[r], returned.at[r], back_recv.at[r]).wait()
        for q in range(DAYS):
            tile = returned[r, q * BANDS : q * BANDS + 8].reshape(LANES, LANES)
            tile = tile.astype(jnp.float32).T.reshape(4, 2, 2, SEG, LANES)
            for g in range(4):
                partner[:, :, q, :, g * LANES : (g + 1) * LANES] = tile[g]
        rest = jnp.concatenate(
            [
                returned[r, q * BANDS + 8 : (q + 1) * BANDS].reshape(PIECE, LANES)
                for q in range(DAYS)
            ],
            axis=0,
        )
        rest = rest.astype(jnp.float32).T
        for q in range(DAYS):
            piece = jnp.zeros((PIECE, LANES), jnp.float32)
            for g in range(4):
                moved = rest[g * PIECE : (g + 1) * PIECE]
                if g != q:
                    moved = pltpu.roll(moved, (PIECE * (g - q)) % LANES, 1)
                piece = jnp.where(quarter == g, moved, piece)
            partner[:, :, q, :, WHOLE:] = piece.reshape(2, 2, SEG, LANES)

        def correlate(q, sums):
            sums = list(sums)
            for seg in range(SEG):
                x_re, x_im = own[0, q, seg], own[1, q, seg]
                for j in range(2):
                    y_re = partner[0, j, q, seg : seg + 1, :]
                    y_im = partner[1, j, q, seg : seg + 1, :]
                    sums[2 * j] = sums[2 * j] + x_re * y_re + x_im * y_im
                    sums[2 * j + 1] = sums[2 * j + 1] + x_im * y_re - x_re * y_im
            return tuple(sums)

        zero = jnp.zeros((SPB, NFREQ), jnp.float32)
        sums = lax.fori_loop(0, DAYS, correlate, (zero,) * 4)
        for j in range(2):
            for c in range(2):
                cross[j * SPB : (j + 1) * SPB, c * NFREQ : (c + 1) * NFREQ] = sums[2 * j + c]
        spectrum = cross[...]
        high = spectrum.astype(jnp.bfloat16)
        low = (spectrum - high.astype(jnp.float32)).astype(jnp.bfloat16)
        raw = dot(high, table[0]) + dot(low, table[0]) + dot(high, table[1])
        for j in range(2):
            square = jnp.zeros((SEG, LANES), jnp.float32)
            for c in range(2):
                for q in range(DAYS):
                    for t in range(TILES):
                        y = partner[c, j, q, :, t * LANES : (t + 1) * LANES]
                        square = square + y * y
            energy_j = jnp.sum(square, axis=1, keepdims=True)
            energy_j = jnp.sum(energy_j, axis=0, keepdims=True) / count + EPS
            scale = 1.0 / (jnp.sqrt(energy_j * energy_i) * np.float32(np.sqrt(count)))
            out_ref[r, j] = (raw[j * SPB : (j + 1) * SPB] * scale).astype(jnp.bfloat16)

    @pl.when(keeps_own)
    def _():
        rest_sent = sent.at[pl.ds(0, KEPT - 1)]
        pltpu.make_async_copy(rest_sent, rest_sent, first_send).wait()

    @pl.when(jnp.logical_not(keeps_own))
    def _():
        pltpu.make_async_copy(sent, sent, first_send).wait()

    @pl.when(is_keeper)
    def _():
        for r in range(ROUNDS):
            rest_sent = picked.at[r, pl.ds(0, BLOCKS - 1)]
            pltpu.make_async_copy(rest_sent, rest_sent, back_send).wait()

    rest_sent = spectra.at[pl.ds(0, DAYS - 1)]
    pltpu.make_async_copy(rest_sent, rest_sent, own_send).wait()


def per_device(spectra, pairing, station_slot):
    x = spectra.reshape(SPB * SEG, 2, NFREQ)
    hbm = pl.BlockSpec(memory_space=pltpu.HBM)
    dma = pltpu.SemaphoreType.DMA
    f32, bf16 = jnp.float32, jnp.bfloat16
    return pl.pallas_call(
        kernel,
        out_shape=jax.ShapeDtypeStruct((ROUNDS, 2, SPB, LAGS), bf16),
        in_specs=[hbm] * 4,
        out_specs=pl.BlockSpec(memory_space=pltpu.VMEM),
        scratch_shapes=[
            pltpu.VMEM((DAYS,) + x.shape, bf16),
            pltpu.SMEM(pairing.shape, jnp.int32),
            pltpu.SMEM(station_slot.shape, jnp.int32),
            pltpu.VMEM((2, SPB, SEG, NFREQ), f32),
            pltpu.VMEM((2, DAYS, SEG, SPB, NFREQ), f32),
            pltpu.VMEM((KEPT, ROWS, LANES), bf16),
            pltpu.VMEM((BLOCKS, ROWS, LANES), bf16),
            pltpu.VMEM((ROUNDS, BLOCKS, ROWS, LANES), bf16),
            pltpu.VMEM((ROUNDS, KEPT, ROWS, LANES), bf16),
            pltpu.VMEM((2, 2, DAYS, SEG, NFREQ), f32),
            pltpu.VMEM((2 * SPB, 2 * NFREQ), f32),
            pltpu.VMEM((2, 2 * NFREQ, LAGS), bf16),
            dma((4,)), dma, dma, dma, dma((ROUNDS,)), dma, dma((DAYS - 1,)),
        ],
        compiler_params=pltpu.CompilerParams(
            collective_id=0, has_side_effects=True, vmem_limit_bytes=63 * 1024 * 1024
        ),
        name="correlate",
    )(x, pairing, station_slot, jnp.asarray(lag_table()))


def solution(mesh):
    in_specs = (P("sta", "day", None, None), P(), P())
    out_specs = P(None, "day", "sta", None)
    return jax.shard_map(
        per_device, mesh=mesh, in_specs=in_specs, out_specs=out_specs, check_vma=False
    )
```

```python
import functools

import jax
import jax.numpy as jnp
import ml_dtypes
import numpy as np
from jax import lax
from jax.experimental import pallas as pl
from jax.experimental.pallas import tpu as pltpu
from jax.sharding import PartitionSpec as P

BIN_LO = 60
SEGLEN = 6000
LAGS = 512
ROUNDS = 3
EPS = 1e-06
NFREQ = 640
SPB = 8
SEG = 8
DAYS = 4
BLOCKS = 64
PLANES = 8
WIDE = 8
BANDS = 8
GROUPS = 5
ROWS = 4
HALVES = 2
NEAR = 4
LANES = 128
PIECE = 32
TILES = NFREQ // LANES
WHOLE = 512
MESH = pl.DeviceIdType.MESH


def lag_table():
    bins = BIN_LO + np.arange(NFREQ, dtype=np.int64)
    shifts = np.arange(LAGS, dtype=np.int64) - LAGS // 2
    turns = np.mod(bins[:, None] * shifts[None, :], SEGLEN)
    angle = 2.0 * np.pi / SEGLEN * turns
    table = np.concatenate([np.cos(angle), -np.sin(angle)], axis=0).astype(np.float32)
    high = table.astype(ml_dtypes.bfloat16)
    low = (table - high.astype(np.float32)).astype(ml_dtypes.bfloat16)
    return np.stack([high, low])


def outward(k, half):
    return half + (k + 1) // 2 * (1 - 2 * (k % 2))


def far_first(sta, k):
    plane = (sta // WIDE + outward(k // WIDE, PLANES // 2)) % PLANES
    return plane * WIDE + (sta % WIDE + k % WIDE + 1) % WIDE


def kernel(
    x_hbm, pairing_hbm, slot_hbm, table_hbm, out_ref,
    spectra, pairing_ref, slot_ref, natural, own, sent, banded, picked, returned, partner, cross, table,
    load_sem, first_send, first_recv, back_send, back_recv, own_send, own_recv,
):
    sta, day = lax.axis_index("sta"), lax.axis_index("day")
    plane, band = sta // WIDE, sta % WIDE
    origin = (plane + band) % DAYS
    keeps_own = origin == day

    barrier = pltpu.get_barrier_semaphore()

    def greet(place, to_day):
        pl.semaphore_signal(barrier, inc=1, device_id=(place, to_day), device_id_type=MESH)

    def greet_block(k, carry):
        greet(far_first(sta, k), origin)
        return carry

    lax.fori_loop(0, BLOCKS - 1, greet_block, 0, unroll=7)

    @pl.when(jnp.logical_not(keeps_own))
    def _():
        greet(sta, origin)

    for k in range(1, DAYS):
        greet(sta, (day + k) % DAYS)

    loads = [
        pltpu.make_async_copy(source, target, load_sem.at[i])
        for i, (source, target) in enumerate(
            [(x_hbm, spectra.at[day]), (slot_hbm, slot_ref), (pairing_hbm, pairing_ref), (table_hbm, table)]
        )
    ]
    for load in loads:
        load.start()

    for load in loads[:2]:
        load.wait()

    def split(day_from):
        for c in range(2):
            part = spectra[day_from, :, c, :].astype(jnp.float32)
            natural[c] = part.reshape(SPB, SEG, NFREQ)

    split(day)
    slots = [slot_ref[sta * SPB + i] for i in range(SPB)]
    order = []
    for j in range(SPB):
        at = jnp.int32(0)
        for i in range(1, SPB):
            at = jnp.where(slots[i] == j, i, at)
        order.append(at)
    pairs = [
        jnp.concatenate(
            [natural[c, order[2 * to + j]] for c in range(2) for j in range(2)], axis=0
        )
        for to in range(DAYS)
    ]
    quarter = lax.broadcasted_iota(jnp.int32, (PIECE, LANES), 1) // PIECE
    for to in range(DAYS):
        tile = jnp.concatenate(
            [pairs[to][:, g * LANES : (g + 1) * LANES] for g in range(4)], axis=0
        )
        tile = tile.T.astype(jnp.bfloat16).reshape(BANDS, GROUPS - 1, ROWS, LANES)
        sent[to * BANDS : (to + 1) * BANDS, : GROUPS - 1] = tile
    rest = []
    for g in range(4):
        piece = jnp.zeros((PIECE, LANES), jnp.float32)
        for to in range(DAYS):
            moved = pairs[to][:, WHOLE:]
            if to != g:
                moved = pltpu.roll(moved, (PIECE * (to - g)) % LANES, 1)
            piece = jnp.where(quarter == to, moved, piece)
        rest.append(piece)
    rest = jnp.concatenate(rest, axis=0).T.astype(jnp.bfloat16)
    for to in range(DAYS):
        tile = rest[to * PIECE : (to + 1) * PIECE].reshape(BANDS, ROWS, LANES)
        sent[to * BANDS : (to + 1) * BANDS, GROUPS - 1] = tile

    loads[2].wait()
    greetings = BLOCKS + DAYS - 1 - jnp.where(keeps_own, 1, 0)
    pl.semaphore_wait(barrier, greetings)

    beside = day + 1 - 2 * (day % 2)
    across = (day + 2) % DAYS

    def send_own(from_day, to_day, i):
        pltpu.make_async_remote_copy(
            src_ref=spectra.at[from_day], dst_ref=spectra.at[from_day], send_sem=own_send, recv_sem=own_recv.at[i],
            device_id=(sta, to_day), device_id_type=MESH,
        ).start()

    def wait_own(i):
        pltpu.make_async_copy(spectra.at[0], spectra.at[0], own_recv.at[i]).wait()

    def keep(from_day, square):
        for c in range(2):
            for seg in range(SEG):
                x = natural[c, :, seg, :]
                own[c, from_day, seg] = x
                for t in range(TILES):
                    x_t = x[:, t * LANES : (t + 1) * LANES]
                    square = square + x_t * x_t
        return square

    send_own(day, across, 0)
    send_own(day, beside, 1)

    def send_first(k, carry):
        to_plane = (plane + outward(k // WIDE, PLANES // 2)) % PLANES
        to_band = (day + PLANES - to_plane) % DAYS + k % HALVES * DAYS
        to = k // HALVES % DAYS
        place = to_plane * WIDE + to_band

        @pl.when(jnp.logical_or(place != sta, to != day))
        def _():
            pltpu.make_async_remote_copy(
                src_ref=sent.at[to * BANDS + to_band], dst_ref=banded.at[sta],
                send_sem=first_send, recv_sem=first_recv, device_id=(place, to), device_id_type=MESH,
            ).start()

        return carry

    lax.fori_loop(0, BLOCKS, send_first, 0, unroll=8)

    @pl.when(keeps_own)
    def _():
        pltpu.make_async_copy(sent.at[day * BANDS + band], banded.at[sta], first_recv).start()

    square = keep(day, jnp.zeros((SPB, LANES), jnp.float32))
    wait_own(1)
    split(beside)
    square = keep(beside, square)
    wait_own(0)
    send_own(across, beside, 2)
    split(across)
    square = keep(across, square)

    side = 2 * (day % 2) - 1
    at = origin * BANDS + band
    pltpu.make_async_copy(banded, banded, first_recv).wait()
    for r in range(ROUNDS):
        for i, offset in enumerate((2, 1, -1, 0)):
            first_block = (plane + PLANES + offset * side) % PLANES * WIDE
            for k in range(WIDE):
                picked[r, i * WIDE + k] = banded[pairing_ref[r, first_block + k]]

            def send_back(k, carry):
                wide = (band + k + 1) % WIDE
                pltpu.make_async_remote_copy(
                    src_ref=picked.at[r, i * WIDE + wide], dst_ref=returned.at[r, at],
                    send_sem=back_send, recv_sem=back_recv.at[r],
                    device_id=(first_block + wide, day), device_id_type=MESH,
                ).start()
                return carry

            if offset:
                lax.fori_loop(0, WIDE, send_back, 0, unroll=True)
            else:
                pltpu.make_async_copy(
                    picked.at[r, i * WIDE + band], returned.at[r, at], back_recv.at[r]
                ).start()
                lax.fori_loop(0, WIDE - 1, send_back, 0, unroll=True)

    wait_own(2)
    last = (beside + 2) % DAYS
    split(last)
    square = keep(last, square)
    count = float(SEG * DAYS * 2 * NFREQ)
    energy_i = jnp.sum(square, axis=1, keepdims=True) / count + EPS

    loads[3].wait()
    dot = functools.partial(jnp.dot, preferred_element_type=jnp.float32)
    for r in range(ROUNDS):
        pltpu.make_async_copy(returned.at[r], returned.at[r], back_recv.at[r]).wait()
        for q in range(DAYS):
            tile = returned[r, q * BANDS : (q + 1) * BANDS, : GROUPS - 1].reshape(LANES, LANES)
            tile = tile.astype(jnp.float32).T.reshape(4, 2, 2, SEG, LANES)
            for g in range(4):
                partner[:, :, q, :, g * LANES : (g + 1) * LANES] = tile[g]
        rest = jnp.concatenate(
            [
                returned[r, q * BANDS : (q + 1) * BANDS, GROUPS - 1].reshape(PIECE, LANES)
                for q in range(DAYS)
            ],
            axis=0,
        )
        rest = rest.astype(jnp.float32).T
        for q in range(DAYS):
            piece = jnp.zeros((PIECE, LANES), jnp.float32)
            for g in range(4):
                moved = rest[g * PIECE : (g + 1) * PIECE]
                if g != q:
                    moved = pltpu.roll(moved, (PIECE * (g - q)) % LANES, 1)
                piece = jnp.where(quarter == g, moved, piece)
            partner[:, :, q, :, WHOLE:] = piece.reshape(2, 2, SEG, LANES)

        def correlate(q, sums):
            sums = list(sums)
            for seg in range(SEG):
                x_re, x_im = own[0, q, seg], own[1, q, seg]
                for j in range(2):
                    y_re = partner[0, j, q, seg : seg + 1, :]
                    y_im = partner[1, j, q, seg : seg + 1, :]
                    sums[2 * j] = sums[2 * j] + x_re * y_re + x_im * y_im
                    sums[2 * j + 1] = sums[2 * j + 1] + x_im * y_re - x_re * y_im
            return tuple(sums)

        zero = jnp.zeros((SPB, NFREQ), jnp.float32)
        sums = lax.fori_loop(0, DAYS, correlate, (zero,) * 4)
        for j in range(2):
            for c in range(2):
                cross[j * SPB : (j + 1) * SPB, c * NFREQ : (c + 1) * NFREQ] = sums[2 * j + c]
        spectrum = cross[...]
        high = spectrum.astype(jnp.bfloat16)
        low = (spectrum - high.astype(jnp.float32)).astype(jnp.bfloat16)
        raw = dot(high, table[0]) + dot(low, table[0]) + dot(high, table[1])
        for j in range(2):
            square = jnp.zeros((SEG, LANES), jnp.float32)
            for c in range(2):
                for q in range(DAYS):
                    for t in range(TILES):
                        y = partner[c, j, q, :, t * LANES : (t + 1) * LANES]
                        square = square + y * y
            energy_j = jnp.sum(square, axis=1, keepdims=True)
            energy_j = jnp.sum(energy_j, axis=0, keepdims=True) / count + EPS
            scale = 1.0 / (jnp.sqrt(energy_j * energy_i) * np.float32(np.sqrt(count)))
            out_ref[r, j] = (raw[j * SPB : (j + 1) * SPB] * scale).astype(jnp.bfloat16)

    tiles = DAYS * BANDS
    pltpu.make_async_copy(sent, sent, first_send).wait()
    rest_sent = sent.at[pl.ds(0, tiles - 1)]
    pltpu.make_async_copy(rest_sent, rest_sent, first_send).wait()

    @pl.when(jnp.logical_not(keeps_own))
    def _():
        pltpu.make_async_copy(sent.at[0], sent.at[0], first_send).wait()

    for r in range(ROUNDS):
        rest_sent = picked.at[r, pl.ds(0, NEAR * WIDE - 1)]
        pltpu.make_async_copy(rest_sent, rest_sent, back_send).wait()
    rest_sent = spectra.at[pl.ds(0, DAYS - 1)]
    pltpu.make_async_copy(rest_sent, rest_sent, own_send).wait()


def per_device(spectra, pairing, station_slot):
    x = spectra.reshape(SPB * SEG, 2, NFREQ)
    hbm = pl.BlockSpec(memory_space=pltpu.HBM)
    dma = pltpu.SemaphoreType.DMA
    f32, bf16 = jnp.float32, jnp.bfloat16
    return pl.pallas_call(
        kernel,
        out_shape=jax.ShapeDtypeStruct((ROUNDS, 2, SPB, LAGS), bf16),
        in_specs=[hbm] * 4,
        out_specs=pl.BlockSpec(memory_space=pltpu.VMEM),
        scratch_shapes=[
            pltpu.VMEM((DAYS,) + x.shape, bf16),
            pltpu.SMEM(pairing.shape, jnp.int32),
            pltpu.SMEM(station_slot.shape, jnp.int32),
            pltpu.VMEM((2, SPB, SEG, NFREQ), f32),
            pltpu.VMEM((2, DAYS, SEG, SPB, NFREQ), f32),
            pltpu.VMEM((DAYS * BANDS, GROUPS, ROWS, LANES), bf16),
            pltpu.VMEM((BLOCKS, GROUPS, ROWS, LANES), bf16),
            pltpu.VMEM((ROUNDS, NEAR * WIDE, GROUPS, ROWS, LANES), bf16),
            pltpu.VMEM((ROUNDS, DAYS * BANDS, GROUPS, ROWS, LANES), bf16),
            pltpu.VMEM((2, 2, DAYS, SEG, NFREQ), f32),
            pltpu.VMEM((2 * SPB, 2 * NFREQ), f32),
            pltpu.VMEM((2, 2 * NFREQ, LAGS), bf16),
            dma((4,)), dma, dma, dma, dma((ROUNDS,)), dma, dma((DAYS - 1,)),
        ],
        compiler_params=pltpu.CompilerParams(
            collective_id=0, has_side_effects=True, vmem_limit_bytes=63 * 1024 * 1024
        ),
        name="correlate",
    )(x, pairing, station_slot, jnp.asarray(lag_table()))


def solution(mesh):
    in_specs = (P("sta", "day", None, None), P(), P())
    out_specs = P(None, "day", "sta", None)
    return jax.shard_map(
        per_device, mesh=mesh, in_specs=in_specs, out_specs=out_specs, check_vma=False
    )
```

```python
import functools

import jax
import jax.numpy as jnp
import ml_dtypes
import numpy as np
from jax import lax
from jax.experimental import pallas as pl
from jax.experimental.pallas import tpu as pltpu
from jax.sharding import PartitionSpec as P

BIN_LO = 60
SEGLEN = 6000
LAGS = 512
ROUNDS = 3
EPS = 1e-06
NFREQ = 640
SPB = 8
SEG = 8
DAYS = 4
BLOCKS = 64
PLANES = 8
WIDE = 8
BANDS = 8
GROUPS = 5
ROWS = 4
HALVES = 2
NEAR = 4
LANES = 128
PIECE = 32
TILES = NFREQ // LANES
WHOLE = 512
MESH = pl.DeviceIdType.MESH


def lag_table():
    bins = BIN_LO + np.arange(NFREQ, dtype=np.int64)
    shifts = np.arange(LAGS, dtype=np.int64) - LAGS // 2
    turns = np.mod(bins[:, None] * shifts[None, :], SEGLEN)
    angle = 2.0 * np.pi / SEGLEN * turns
    table = np.concatenate([np.cos(angle), -np.sin(angle)], axis=0).astype(np.float32)
    high = table.astype(ml_dtypes.bfloat16)
    low = (table - high.astype(np.float32)).astype(ml_dtypes.bfloat16)
    return np.stack([high, low])


def outward(k, half):
    return half + (k + 1) // 2 * (1 - 2 * (k % 2))


def far_first(sta, k):
    plane = (sta // WIDE + outward(k // WIDE, PLANES // 2)) % PLANES
    return plane * WIDE + (sta % WIDE + k % WIDE + 1) % WIDE


def kernel(
    x_hbm, plan_hbm, table_hbm, out_ref,
    spectra, plan_ref, natural, own, sent, banded, picked, returned, partner, cross, table,
    load_sem, first_send, first_recv, back_send, back_recv, own_send, own_recv,
):
    sta, day = lax.axis_index("sta"), lax.axis_index("day")
    plane, band = sta // WIDE, sta % WIDE
    origin = (plane + band) % DAYS
    keeps_own = origin == day

    barrier = pltpu.get_barrier_semaphore()

    def greet(place, to_day):
        pl.semaphore_signal(barrier, inc=1, device_id=(place, to_day), device_id_type=MESH)

    def greet_block(k, carry):
        greet(far_first(sta, k), origin)
        return carry

    lax.fori_loop(0, BLOCKS - 1, greet_block, 0, unroll=7)

    @pl.when(jnp.logical_not(keeps_own))
    def _():
        greet(sta, origin)

    for k in range(1, DAYS):
        greet(sta, (day + k) % DAYS)

    loads = [
        pltpu.make_async_copy(source, target, load_sem.at[i])
        for i, (source, target) in enumerate(
            [(x_hbm, spectra.at[day]), (plan_hbm, plan_ref), (table_hbm, table)]
        )
    ]
    for load in loads:
        load.start()

    for load in loads[:2]:
        load.wait()

    def split(day_from):
        for c in range(2):
            part = spectra[day_from, :, c, :].astype(jnp.float32)
            natural[c] = part.reshape(SPB, SEG, NFREQ)

    split(day)
    slots = [plan_ref[ROUNDS, sta * SPB + i] for i in range(SPB)]
    order = []
    for j in range(SPB):
        at = jnp.int32(0)
        for i in range(1, SPB):
            at = jnp.where(slots[i] == j, i, at)
        order.append(at)
    pairs = [
        jnp.concatenate(
            [natural[c, order[2 * to + j]] for c in range(2) for j in range(2)], axis=0
        )
        for to in range(DAYS)
    ]
    quarter = lax.broadcasted_iota(jnp.int32, (PIECE, LANES), 1) // PIECE
    for to in range(DAYS):
        tile = jnp.concatenate(
            [pairs[to][:, g * LANES : (g + 1) * LANES] for g in range(4)], axis=0
        )
        tile = tile.T.astype(jnp.bfloat16).reshape(BANDS, GROUPS - 1, ROWS, LANES)
        sent[to * BANDS : (to + 1) * BANDS, : GROUPS - 1] = tile
    rest = []
    for g in range(4):
        piece = jnp.zeros((PIECE, LANES), jnp.float32)
        for to in range(DAYS):
            moved = pairs[to][:, WHOLE:]
            if to != g:
                moved = pltpu.roll(moved, (PIECE * (to - g)) % LANES, 1)
            piece = jnp.where(quarter == to, moved, piece)
        rest.append(piece)
    rest = jnp.concatenate(rest, axis=0).T.astype(jnp.bfloat16)
    for to in range(DAYS):
        tile = rest[to * PIECE : (to + 1) * PIECE].reshape(BANDS, ROWS, LANES)
        sent[to * BANDS : (to + 1) * BANDS, GROUPS - 1] = tile

    greetings = BLOCKS + DAYS - 1 - jnp.where(keeps_own, 1, 0)
    pl.semaphore_wait(barrier, greetings)

    beside = day + 1 - 2 * (day % 2)
    across = (day + 2) % DAYS

    def send_own(from_day, to_day, i, part=slice(None)):
        pltpu.make_async_remote_copy(
            src_ref=spectra.at[from_day, part], dst_ref=spectra.at[from_day, part], send_sem=own_send, recv_sem=own_recv.at[i],
            device_id=(sta, to_day), device_id_type=MESH,
        ).start()

    def wait_own(i):
        pltpu.make_async_copy(spectra.at[0], spectra.at[0], own_recv.at[i]).wait()

    def keep(from_day, square):
        for c in range(2):
            for seg in range(SEG):
                x = natural[c, :, seg, :]
                own[c, from_day, seg] = x
                for t in range(TILES):
                    x_t = x[:, t * LANES : (t + 1) * LANES]
                    square = square + x_t * x_t
        return square

    send_own(day, beside, 1)

    def send_first(k, carry):
        to_plane = (plane + 1 + k // WIDE) % PLANES
        turn = (k + band) % WIDE
        to_band = (day + PLANES - to_plane) % DAYS + turn % HALVES * DAYS
        to = turn // HALVES
        place = to_plane * WIDE + to_band

        @pl.when(jnp.logical_or(place != sta, to != day))
        def _():
            pltpu.make_async_remote_copy(
                src_ref=sent.at[to * BANDS + to_band], dst_ref=banded.at[sta],
                send_sem=first_send, recv_sem=first_recv, device_id=(place, to), device_id_type=MESH,
            ).start()

        return carry

    for i in range(PLANES):
        lax.fori_loop(i * WIDE, (i + 1) * WIDE, send_first, 0, unroll=True)
        send_own(day, across, 0, pl.ds(i * SPB, SPB))

    @pl.when(keeps_own)
    def _():
        pltpu.make_async_copy(sent.at[day * BANDS + band], banded.at[sta], first_recv).start()

    square = keep(day, jnp.zeros((SPB, LANES), jnp.float32))
    wait_own(1)
    split(beside)
    square = keep(beside, square)
    wait_own(0)
    send_own(across, beside, 2)
    split(across)
    square = keep(across, square)

    side = 2 * (day % 2) - 1
    at = origin * BANDS + band
    pltpu.make_async_copy(banded, banded, first_recv).wait()
    for r in range(ROUNDS):
        for i, offset in enumerate((2, 1, -1, 0)):
            first_block = (plane + PLANES + offset * side) % PLANES * WIDE
            for k in range(WIDE):
                picked[r, i * WIDE + k] = banded[plan_ref[r, first_block + k]]

            def send_back(k, carry):
                wide = (band + k + 1) % WIDE
                pltpu.make_async_remote_copy(
                    src_ref=picked.at[r, i * WIDE + wide], dst_ref=returned.at[r, at],
                    send_sem=back_send, recv_sem=back_recv.at[r],
                    device_id=(first_block + wide, day), device_id_type=MESH,
                ).start()
                return carry

            if offset:
                lax.fori_loop(0, WIDE, send_back, 0, unroll=True)
            else:
                pltpu.make_async_copy(
                    picked.at[r, i * WIDE + band], returned.at[r, at], back_recv.at[r]
                ).start()
                lax.fori_loop(0, WIDE - 1, send_back, 0, unroll=True)

    wait_own(2)
    last = (beside + 2) % DAYS
    split(last)
    square = keep(last, square)
    count = float(SEG * DAYS * 2 * NFREQ)
    energy_i = jnp.sum(square, axis=1, keepdims=True) / count + EPS

    loads[2].wait()
    dot = functools.partial(jnp.dot, preferred_element_type=jnp.float32)
    for r in range(ROUNDS):
        pltpu.make_async_copy(returned.at[r], returned.at[r], back_recv.at[r]).wait()
        for q in range(DAYS):
            tile = returned[r, q * BANDS : (q + 1) * BANDS, : GROUPS - 1].reshape(LANES, LANES)
            tile = tile.astype(jnp.float32).T.reshape(4, 2, 2, SEG, LANES)
            for g in range(4):
                partner[:, :, q, :, g * LANES : (g + 1) * LANES] = tile[g]
        rest = jnp.concatenate(
            [
                returned[r, q * BANDS : (q + 1) * BANDS, GROUPS - 1].reshape(PIECE, LANES)
                for q in range(DAYS)
            ],
            axis=0,
        )
        rest = rest.astype(jnp.float32).T
        for q in range(DAYS):
            piece = jnp.zeros((PIECE, LANES), jnp.float32)
            for g in range(4):
                moved = rest[g * PIECE : (g + 1) * PIECE]
                if g != q:
                    moved = pltpu.roll(moved, (PIECE * (g - q)) % LANES, 1)
                piece = jnp.where(quarter == g, moved, piece)
            partner[:, :, q, :, WHOLE:] = piece.reshape(2, 2, SEG, LANES)

        def correlate(q, sums):
            sums = list(sums)
            for seg in range(SEG):
                x_re, x_im = own[0, q, seg], own[1, q, seg]
                for j in range(2):
                    y_re = partner[0, j, q, seg : seg + 1, :]
                    y_im = partner[1, j, q, seg : seg + 1, :]
                    sums[2 * j] = sums[2 * j] + x_re * y_re + x_im * y_im
                    sums[2 * j + 1] = sums[2 * j + 1] + x_im * y_re - x_re * y_im
            return tuple(sums)

        zero = jnp.zeros((SPB, NFREQ), jnp.float32)
        sums = lax.fori_loop(0, DAYS, correlate, (zero,) * 4)
        for j in range(2):
            for c in range(2):
                cross[j * SPB : (j + 1) * SPB, c * NFREQ : (c + 1) * NFREQ] = sums[2 * j + c]
        spectrum = cross[...]
        high = spectrum.astype(jnp.bfloat16)
        low = (spectrum - high.astype(jnp.float32)).astype(jnp.bfloat16)
        raw = dot(high, table[0]) + dot(low, table[0]) + dot(high, table[1])
        for j in range(2):
            square = jnp.zeros((SEG, LANES), jnp.float32)
            for c in range(2):
                for q in range(DAYS):
                    for t in range(TILES):
                        y = partner[c, j, q, :, t * LANES : (t + 1) * LANES]
                        square = square + y * y
            energy_j = jnp.sum(square, axis=1, keepdims=True)
            energy_j = jnp.sum(energy_j, axis=0, keepdims=True) / count + EPS
            scale = 1.0 / (jnp.sqrt(energy_j * energy_i) * np.float32(np.sqrt(count)))
            out_ref[r, j] = (raw[j * SPB : (j + 1) * SPB] * scale).astype(jnp.bfloat16)

    tiles = DAYS * BANDS
    pltpu.make_async_copy(sent, sent, first_send).wait()
    rest_sent = sent.at[pl.ds(0, tiles - 1)]
    pltpu.make_async_copy(rest_sent, rest_sent, first_send).wait()

    @pl.when(jnp.logical_not(keeps_own))
    def _():
        pltpu.make_async_copy(sent.at[0], sent.at[0], first_send).wait()

    for r in range(ROUNDS):
        rest_sent = picked.at[r, pl.ds(0, NEAR * WIDE - 1)]
        pltpu.make_async_copy(rest_sent, rest_sent, back_send).wait()
    rest_sent = spectra.at[pl.ds(0, DAYS - 1)]
    pltpu.make_async_copy(rest_sent, rest_sent, own_send).wait()


def per_device(spectra, pairing, station_slot):
    x = spectra.reshape(SPB * SEG, 2, NFREQ)
    wide = jnp.pad(pairing, ((0, 0), (0, station_slot.size - BLOCKS)))
    plan = jnp.concatenate([wide, station_slot[None]], axis=0)
    hbm = pl.BlockSpec(memory_space=pltpu.HBM)
    dma = pltpu.SemaphoreType.DMA
    f32, bf16 = jnp.float32, jnp.bfloat16
    return pl.pallas_call(
        kernel,
        out_shape=jax.ShapeDtypeStruct((ROUNDS, 2, SPB, LAGS), bf16),
        in_specs=[hbm] * 3,
        out_specs=pl.BlockSpec(memory_space=pltpu.VMEM),
        scratch_shapes=[
            pltpu.VMEM((DAYS,) + x.shape, bf16),
            pltpu.SMEM(plan.shape, jnp.int32),
            pltpu.VMEM((2, SPB, SEG, NFREQ), f32),
            pltpu.VMEM((2, DAYS, SEG, SPB, NFREQ), f32),
            pltpu.VMEM((DAYS * BANDS, GROUPS, ROWS, LANES), bf16),
            pltpu.VMEM((BLOCKS, GROUPS, ROWS, LANES), bf16),
            pltpu.VMEM((ROUNDS, NEAR * WIDE, GROUPS, ROWS, LANES), bf16),
            pltpu.VMEM((ROUNDS, DAYS * BANDS, GROUPS, ROWS, LANES), bf16),
            pltpu.VMEM((2, 2, DAYS, SEG, NFREQ), f32),
            pltpu.VMEM((2 * SPB, 2 * NFREQ), f32),
            pltpu.VMEM((2, 2 * NFREQ, LAGS), bf16),
            dma((3,)), dma, dma, dma, dma((ROUNDS,)), dma, dma((DAYS - 1,)),
        ],
        compiler_params=pltpu.CompilerParams(
            collective_id=0, has_side_effects=True, vmem_limit_bytes=55168 * 1024
        ),
        name="correlate",
    )(x, plan, jnp.asarray(lag_table()))


def solution(mesh):
    in_specs = (P("sta", "day", None, None), P(), P())
    out_specs = P(None, "day", "sta", None)
    return jax.shard_map(
        per_device, mesh=mesh, in_specs=in_specs, out_specs=out_specs, check_vma=False
    )
```

```python
import functools

import jax
import jax.numpy as jnp
import ml_dtypes
import numpy as np
from jax import lax
from jax.experimental import pallas as pl
from jax.experimental.pallas import tpu as pltpu
from jax.sharding import PartitionSpec as P

BIN_LO = 60
SEGLEN = 6000
LAGS = 512
ROUNDS = 3
EPS = 1e-06
NFREQ = 640
SPB = 8
SEG = 8
DAYS = 4
BLOCKS = 64
PLANES = 8
WIDE = 8
BANDS = 8
GROUPS = 5
ROWS = 4
HALVES = 2
NEAR = 4
LANES = 128
PIECE = 32
TILES = NFREQ // LANES
WHOLE = 512
MESH = pl.DeviceIdType.MESH
ORDER = sorted(
    ((r, i) for r in range(ROUNDS) for i in range(NEAR)), key=lambda at: (at[0], at[1])
)


def lag_table():
    bins = BIN_LO + np.arange(NFREQ, dtype=np.int64)
    halves = 2 * np.arange(LAGS // 2, dtype=np.int64) + 1
    turns = np.mod(bins[:, None] * halves[None, :], 2 * SEGLEN)
    angle = np.pi / SEGLEN * turns
    table = np.stack([np.cos(angle), np.sin(angle)]).astype(np.float32)
    high = table.astype(ml_dtypes.bfloat16)
    low = (table - high.astype(np.float32)).astype(ml_dtypes.bfloat16)
    return np.stack([high, low])


def outward(k, half):
    return half + (k + 1) // 2 * (1 - 2 * (k % 2))


def far_first(sta, k):
    plane = (sta // WIDE + outward(k // WIDE, PLANES // 2)) % PLANES
    return plane * WIDE + (sta % WIDE + k % WIDE + 1) % WIDE


def kernel(
    x_hbm, plan_hbm, table_hbm, out_ref,
    spectra, plan_ref, natural, own, sent, banded, picked, returned, partner, cross, table,
    load_sem, first_send, first_recv, back_send, back_recv, own_send, own_recv,
):
    sta, day = lax.axis_index("sta"), lax.axis_index("day")
    plane, band = sta // WIDE, sta % WIDE
    origin = (plane + band) % DAYS
    keeps_own = origin == day

    barrier = pltpu.get_barrier_semaphore()

    def greet(place, to_day):
        pl.semaphore_signal(barrier, inc=1, device_id=(place, to_day), device_id_type=MESH)

    def greet_block(k, carry):
        greet(far_first(sta, k), origin)
        return carry

    lax.fori_loop(0, BLOCKS - 1, greet_block, 0, unroll=7)

    @pl.when(jnp.logical_not(keeps_own))
    def _():
        greet(sta, origin)

    for k in range(1, DAYS):
        greet(sta, (day + k) % DAYS)

    loads = [
        pltpu.make_async_copy(source, target, load_sem.at[i])
        for i, (source, target) in enumerate(
            [(x_hbm, spectra.at[day]), (plan_hbm, plan_ref), (table_hbm, table)]
        )
    ]
    for load in loads:
        load.start()

    for load in loads[:2]:
        load.wait()

    def split(day_from):
        for c in range(2):
            part = spectra[day_from, :, c, :].astype(jnp.float32)
            natural[c] = part.reshape(SPB, SEG, NFREQ)

    split(day)
    slots = [plan_ref[ROUNDS, sta * SPB + i] for i in range(SPB)]
    order = []
    for j in range(SPB):
        at = jnp.int32(0)
        for i in range(1, SPB):
            at = jnp.where(slots[i] == j, i, at)
        order.append(at)
    pairs = [
        jnp.concatenate(
            [natural[c, order[2 * to + j]] for c in range(2) for j in range(2)], axis=0
        )
        for to in range(DAYS)
    ]
    quarter = lax.broadcasted_iota(jnp.int32, (PIECE, LANES), 1) // PIECE
    for to in range(DAYS):
        tile = jnp.concatenate(
            [pairs[to][:, g * LANES : (g + 1) * LANES] for g in range(4)], axis=0
        )
        tile = tile.T.astype(jnp.bfloat16).reshape(BANDS, GROUPS - 1, ROWS, LANES)
        sent[to * BANDS : (to + 1) * BANDS, : GROUPS - 1] = tile
    rest = []
    for g in range(4):
        piece = jnp.zeros((PIECE, LANES), jnp.float32)
        for to in range(DAYS):
            moved = pairs[to][:, WHOLE:]
            if to != g:
                moved = pltpu.roll(moved, (PIECE * (to - g)) % LANES, 1)
            piece = jnp.where(quarter == to, moved, piece)
        rest.append(piece)
    rest = jnp.concatenate(rest, axis=0).T.astype(jnp.bfloat16)
    for to in range(DAYS):
        tile = rest[to * PIECE : (to + 1) * PIECE].reshape(BANDS, ROWS, LANES)
        sent[to * BANDS : (to + 1) * BANDS, GROUPS - 1] = tile

    greetings = BLOCKS + DAYS - 1 - jnp.where(keeps_own, 1, 0)
    pl.semaphore_wait(barrier, greetings)

    beside = day + 1 - 2 * (day % 2)
    across = (day + 2) % DAYS

    def send_own(from_day, to_day, i, part=slice(None)):
        pltpu.make_async_remote_copy(
            src_ref=spectra.at[from_day, part], dst_ref=spectra.at[from_day, part], send_sem=own_send, recv_sem=own_recv.at[i],
            device_id=(sta, to_day), device_id_type=MESH,
        ).start()

    def wait_own(i):
        pltpu.make_async_copy(spectra.at[0], spectra.at[0], own_recv.at[i]).wait()

    def keep(from_day, square):
        for c in range(2):
            for seg in range(SEG):
                x = natural[c, :, seg, :]
                own[c, from_day, seg] = x
                for t in range(TILES):
                    x_t = x[:, t * LANES : (t + 1) * LANES]
                    square = square + x_t * x_t
        return square

    send_own(day, beside, 1)

    def send_first(k, carry):
        to_plane = (plane + 1 + k // WIDE) % PLANES
        turn = (k + band) % WIDE
        to_band = (day + PLANES - to_plane) % DAYS + turn % HALVES * DAYS
        to = turn // HALVES
        place = to_plane * WIDE + to_band

        @pl.when(jnp.logical_or(place != sta, to != day))
        def _():
            pltpu.make_async_remote_copy(
                src_ref=sent.at[to * BANDS + to_band], dst_ref=banded.at[sta],
                send_sem=first_send, recv_sem=first_recv, device_id=(place, to), device_id_type=MESH,
            ).start()

        return carry

    for i in range(PLANES):
        lax.fori_loop(i * WIDE, (i + 1) * WIDE, send_first, 0, unroll=True)
        send_own(day, across, 0, pl.ds(i * SPB, SPB))

    @pl.when(keeps_own)
    def _():
        pltpu.make_async_copy(sent.at[day * BANDS + band], banded.at[sta], first_recv).start()

    square = keep(day, jnp.zeros((SPB, LANES), jnp.float32))
    wait_own(1)
    split(beside)
    square = keep(beside, square)
    wait_own(0)
    send_own(across, beside, 2)

    at = origin * BANDS + band
    pltpu.make_async_copy(banded, banded, first_recv).wait()
    first_plane = (plane + PLANES - 2 + day % 2) % PLANES
    wrapped = jnp.maximum(first_plane + NEAR - PLANES, 0)
    for r, i in ORDER:
        to_plane = (first_plane + (NEAR - wrapped + i) % NEAR) % PLANES
        for k in range(WIDE):
            picked[r, i * WIDE + k] = banded[plan_ref[r, to_plane * WIDE + k]]

        def send_back(k, carry):
            wide = (band + k + 1) % WIDE
            pltpu.make_async_remote_copy(
                src_ref=picked.at[r, i * WIDE + wide], dst_ref=returned.at[r, at],
                send_sem=back_send, recv_sem=back_recv.at[r],
                device_id=(to_plane * WIDE + wide, day), device_id_type=MESH,
            ).start()
            return carry

        lax.fori_loop(0, WIDE - 1, send_back, 0, unroll=True)

        @pl.when(to_plane != plane)
        def _():
            send_back(WIDE - 1, 0)

        @pl.when(to_plane == plane)
        def _():
            pltpu.make_async_copy(
                picked.at[r, i * WIDE + band], returned.at[r, at], back_recv.at[r]
            ).start()

    split(across)
    square = keep(across, square)
    wait_own(2)
    last = (beside + 2) % DAYS
    split(last)
    square = keep(last, square)
    count = float(SEG * DAYS * 2 * NFREQ)
    energy_i = jnp.sum(square, axis=1, keepdims=True) / count + EPS

    loads[2].wait()
    dot = functools.partial(jnp.dot, preferred_element_type=jnp.float32)
    bins = BIN_LO + lax.broadcasted_iota(jnp.int32, (SPB, NFREQ), 1)
    half = bins.astype(jnp.float32) * np.float32(np.pi / SEGLEN)
    half_cos, half_sin = jnp.cos(half), jnp.sin(half)
    backward = LANES - 1 - lax.broadcasted_iota(jnp.int32, (2 * SPB, LANES), 1)

    def mirrored(tile):
        return jnp.take_along_axis(tile, backward, axis=1)

    for r in range(ROUNDS):
        pltpu.make_async_copy(returned.at[r], returned.at[r], back_recv.at[r]).wait()
        for q in range(DAYS):
            tile = returned[r, q * BANDS : (q + 1) * BANDS, : GROUPS - 1].reshape(LANES, LANES)
            tile = tile.astype(jnp.float32).T.reshape(4, 2, 2, SEG, LANES)
            for g in range(4):
                partner[:, :, q, :, g * LANES : (g + 1) * LANES] = tile[g]
        rest = jnp.concatenate(
            [
                returned[r, q * BANDS : (q + 1) * BANDS, GROUPS - 1].reshape(PIECE, LANES)
                for q in range(DAYS)
            ],
            axis=0,
        )
        rest = rest.astype(jnp.float32).T
        for q in range(DAYS):
            piece = jnp.zeros((PIECE, LANES), jnp.float32)
            for g in range(4):
                moved = rest[g * PIECE : (g + 1) * PIECE]
                if g != q:
                    moved = pltpu.roll(moved, (PIECE * (g - q)) % LANES, 1)
                piece = jnp.where(quarter == g, moved, piece)
            partner[:, :, q, :, WHOLE:] = piece.reshape(2, 2, SEG, LANES)

        def correlate(q, sums):
            sums = list(sums)
            for seg in range(SEG):
                x_re, x_im = own[0, q, seg], own[1, q, seg]
                for j in range(2):
                    y_re = partner[0, j, q, seg : seg + 1, :]
                    y_im = partner[1, j, q, seg : seg + 1, :]
                    sums[2 * j] = sums[2 * j] + x_re * y_re + x_im * y_im
                    sums[2 * j + 1] = sums[2 * j + 1] + x_im * y_re - x_re * y_im
            return tuple(sums)

        zero = jnp.zeros((SPB, NFREQ), jnp.float32)
        sums = lax.fori_loop(0, DAYS, correlate, (zero,) * 4)
        for j in range(2):
            real, imag = sums[2 * j], sums[2 * j + 1]
            cross[0, j * SPB : (j + 1) * SPB] = real * half_cos + imag * half_sin
            cross[1, j * SPB : (j + 1) * SPB] = imag * half_cos - real * half_sin
        waves = []
        for c in range(2):
            high = cross[c].astype(jnp.bfloat16)
            low = (cross[c] - high.astype(jnp.float32)).astype(jnp.bfloat16)
            both = dot(jnp.concatenate([high, low], axis=0), table[0, c])
            waves.append(both[: 2 * SPB] + both[2 * SPB :] + dot(high, table[1, c]))
        early, late = waves[0] + waves[1], waves[0] - waves[1]
        raw = jnp.concatenate(
            [mirrored(early[:, LANES:]), mirrored(early[:, :LANES]), late], axis=1
        )
        for j in range(2):
            square = jnp.zeros((SEG, LANES), jnp.float32)
            for c in range(2):
                for q in range(DAYS):
                    for t in range(TILES):
                        y = partner[c, j, q, :, t * LANES : (t + 1) * LANES]
                        square = square + y * y
            energy_j = jnp.sum(square, axis=1, keepdims=True)
            energy_j = jnp.sum(energy_j, axis=0, keepdims=True) / count + EPS
            scale = 1.0 / (jnp.sqrt(energy_j * energy_i) * np.float32(np.sqrt(count)))
            out_ref[r, j] = (raw[j * SPB : (j + 1) * SPB] * scale).astype(jnp.bfloat16)

    tiles = DAYS * BANDS
    pltpu.make_async_copy(sent, sent, first_send).wait()
    rest_sent = sent.at[pl.ds(0, tiles - 1)]
    pltpu.make_async_copy(rest_sent, rest_sent, first_send).wait()

    @pl.when(jnp.logical_not(keeps_own))
    def _():
        pltpu.make_async_copy(sent.at[0], sent.at[0], first_send).wait()

    for r in range(ROUNDS):
        rest_sent = picked.at[r, pl.ds(0, NEAR * WIDE - 1)]
        pltpu.make_async_copy(rest_sent, rest_sent, back_send).wait()
    rest_sent = spectra.at[pl.ds(0, DAYS - 1)]
    pltpu.make_async_copy(rest_sent, rest_sent, own_send).wait()


def per_device(spectra, pairing, station_slot):
    x = spectra.reshape(SPB * SEG, 2, NFREQ)
    wide = jnp.pad(pairing, ((0, 0), (0, station_slot.size - BLOCKS)))
    plan = jnp.concatenate([wide, station_slot[None]], axis=0)
    hbm = pl.BlockSpec(memory_space=pltpu.HBM)
    dma = pltpu.SemaphoreType.DMA
    f32, bf16 = jnp.float32, jnp.bfloat16
    return pl.pallas_call(
        kernel,
        out_shape=jax.ShapeDtypeStruct((ROUNDS, 2, SPB, LAGS), bf16),
        in_specs=[hbm] * 3,
        out_specs=pl.BlockSpec(memory_space=pltpu.VMEM),
        scratch_shapes=[
            pltpu.VMEM((DAYS,) + x.shape, bf16),
            pltpu.SMEM(plan.shape, jnp.int32),
            pltpu.VMEM((2, SPB, SEG, NFREQ), f32),
            pltpu.VMEM((2, DAYS, SEG, SPB, NFREQ), f32),
            pltpu.VMEM((DAYS * BANDS, GROUPS, ROWS, LANES), bf16),
            pltpu.VMEM((BLOCKS, GROUPS, ROWS, LANES), bf16),
            pltpu.VMEM((ROUNDS, NEAR * WIDE, GROUPS, ROWS, LANES), bf16),
            pltpu.VMEM((ROUNDS, DAYS * BANDS, GROUPS, ROWS, LANES), bf16),
            pltpu.VMEM((2, 2, DAYS, SEG, NFREQ), f32),
            pltpu.VMEM((2, 2 * SPB, NFREQ), f32),
            pltpu.VMEM((2, 2, NFREQ, LAGS // 2), bf16),
            dma((3,)), dma, dma, dma, dma((ROUNDS,)), dma, dma((DAYS - 1,)),
        ],
        compiler_params=pltpu.CompilerParams(
            collective_id=0, has_side_effects=True, vmem_limit_bytes=55168 * 1024
        ),
        name="correlate",
    )(x, plan, jnp.asarray(lag_table()))


def solution(mesh):
    in_specs = (P("sta", "day", None, None), P(), P())
    out_specs = P(None, "day", "sta", None)
    return jax.shard_map(
        per_device, mesh=mesh, in_specs=in_specs, out_specs=out_specs, check_vma=False
    )
```

```python
import functools

import jax
import jax.numpy as jnp
import ml_dtypes
import numpy as np
from jax import lax
from jax.experimental import pallas as pl
from jax.experimental.pallas import tpu as pltpu
from jax.sharding import PartitionSpec as P

BIN_LO = 60
SEGLEN = 6000
LAGS = 512
ROUNDS = 3
EPS = 1e-06
NFREQ = 640
SPB = 8
SEG = 8
DAYS = 4
BLOCKS = 64
PLANES = 8
WIDE = 8
BANDS = 8
GROUPS = 5
ROWS = 4
HALVES = 2
NEAR = 4
LANES = 128
PIECE = 32
TILES = NFREQ // LANES
WHOLE = 512
MESH = pl.DeviceIdType.MESH


def lag_table():
    bins = BIN_LO + np.arange(NFREQ, dtype=np.int64)
    halves = 2 * np.arange(LAGS // 2, dtype=np.int64) + 1
    turns = np.mod(bins[:, None] * halves[None, :], 2 * SEGLEN)
    angle = np.pi / SEGLEN * turns
    table = np.stack([np.cos(angle), np.sin(angle)]).astype(np.float32)
    high = table.astype(ml_dtypes.bfloat16)
    low = (table - high.astype(np.float32)).astype(ml_dtypes.bfloat16)
    return np.stack([high, low])


def outward(k, half):
    return half + (k + 1) // 2 * (1 - 2 * (k % 2))


def far_first(sta, k):
    plane = (sta // WIDE + outward(k // WIDE, PLANES // 2)) % PLANES
    return plane * WIDE + (sta % WIDE + k % WIDE + 1) % WIDE


def kernel(
    x_hbm, plan_hbm, table_hbm, out_ref,
    spectra, plan_ref, natural, own, sent, banded, picked, returned, partner, cross, table,
    load_sem, first_send, first_recv, back_send, back_recv, own_send, own_recv,
):
    sta, day = lax.axis_index("sta"), lax.axis_index("day")
    plane, band = sta // WIDE, sta % WIDE
    origin = (plane + band) % DAYS
    keeps_own = origin == day

    barrier = pltpu.get_barrier_semaphore()

    def greet(place, to_day):
        pl.semaphore_signal(barrier, inc=1, device_id=(place, to_day), device_id_type=MESH)

    def greet_block(k, carry):
        greet(far_first(sta, k), origin)
        return carry

    lax.fori_loop(0, BLOCKS - 1, greet_block, 0, unroll=7)

    @pl.when(jnp.logical_not(keeps_own))
    def _():
        greet(sta, origin)

    for k in range(1, DAYS):
        greet(sta, (day + k) % DAYS)

    loads = [
        pltpu.make_async_copy(source, target, load_sem.at[i])
        for i, (source, target) in enumerate(
            [(x_hbm, spectra.at[day]), (plan_hbm, plan_ref), (table_hbm, table)]
        )
    ]
    for load in loads:
        load.start()

    for load in loads[:2]:
        load.wait()

    def split(day_from):
        for c in range(2):
            part = spectra[day_from, :, c, :].astype(jnp.float32)
            natural[c] = part.reshape(SPB, SEG, NFREQ)

    split(day)
    slots = [plan_ref[ROUNDS, sta * SPB + i] for i in range(SPB)]
    order = []
    for j in range(SPB):
        at = jnp.int32(0)
        for i in range(1, SPB):
            at = jnp.where(slots[i] == j, i, at)
        order.append(at)
    pairs = [
        jnp.concatenate(
            [natural[c, order[2 * to + j]] for c in range(2) for j in range(2)], axis=0
        )
        for to in range(DAYS)
    ]
    quarter = lax.broadcasted_iota(jnp.int32, (PIECE, LANES), 1) // PIECE
    for to in range(DAYS):
        tile = jnp.concatenate(
            [pairs[to][:, g * LANES : (g + 1) * LANES] for g in range(4)], axis=0
        )
        tile = tile.T.astype(jnp.bfloat16).reshape(BANDS, GROUPS - 1, ROWS, LANES)
        sent[to * BANDS : (to + 1) * BANDS, : GROUPS - 1] = tile
    rest = []
    for g in range(4):
        piece = jnp.zeros((PIECE, LANES), jnp.float32)
        for to in range(DAYS):
            moved = pairs[to][:, WHOLE:]
            if to != g:
                moved = pltpu.roll(moved, (PIECE * (to - g)) % LANES, 1)
            piece = jnp.where(quarter == to, moved, piece)
        rest.append(piece)
    rest = jnp.concatenate(rest, axis=0).T.astype(jnp.bfloat16)
    for to in range(DAYS):
        tile = rest[to * PIECE : (to + 1) * PIECE].reshape(BANDS, ROWS, LANES)
        sent[to * BANDS : (to + 1) * BANDS, GROUPS - 1] = tile

    greetings = BLOCKS + DAYS - 1 - jnp.where(keeps_own, 1, 0)
    pl.semaphore_wait(barrier, greetings)

    beside = day + 1 - 2 * (day % 2)
    across = (day + 2) % DAYS

    def send_own(from_day, to_day, i, part=slice(None)):
        pltpu.make_async_remote_copy(
            src_ref=spectra.at[from_day, part], dst_ref=spectra.at[from_day, part], send_sem=own_send, recv_sem=own_recv.at[i],
            device_id=(sta, to_day), device_id_type=MESH,
        ).start()

    def wait_own(i):
        pltpu.make_async_copy(spectra.at[0], spectra.at[0], own_recv.at[i]).wait()

    def keep(from_day, square):
        for c in range(2):
            for seg in range(SEG):
                x = natural[c, :, seg, :]
                own[c, from_day, seg] = x
                for t in range(TILES):
                    x_t = x[:, t * LANES : (t + 1) * LANES]
                    square = square + x_t * x_t
        return square

    send_own(day, beside, 1)

    def send_first(k, carry):
        step = k // WIDE
        to_plane = PLANES + (step // 2 + 1) * (1 - 2 * (step % 2)) + step // (PLANES - 1) * DAYS
        to_plane = (plane + to_plane) % PLANES
        turn = (k + band) % WIDE
        to_band = (day + PLANES - to_plane) % DAYS + turn % HALVES * DAYS
        to = turn // HALVES
        place = to_plane * WIDE + to_band

        @pl.when(jnp.logical_or(place != sta, to != day))
        def _():
            pltpu.make_async_remote_copy(
                src_ref=sent.at[to * BANDS + to_band], dst_ref=banded.at[sta],
                send_sem=first_send, recv_sem=first_recv, device_id=(place, to), device_id_type=MESH,
            ).start()

        return carry

    for i in range(PLANES):
        lax.fori_loop(i * WIDE, (i + 1) * WIDE, send_first, 0, unroll=True)
        send_own(day, across, 0, pl.ds(i * SPB, SPB))

    @pl.when(keeps_own)
    def _():
        pltpu.make_async_copy(sent.at[day * BANDS + band], banded.at[sta], first_recv).start()

    square = keep(day, jnp.zeros((SPB, LANES), jnp.float32))
    wait_own(1)
    split(beside)
    square = keep(beside, square)
    wait_own(0)
    send_own(across, beside, 2)

    at = origin * BANDS + band
    pltpu.make_async_copy(banded, banded, first_recv).wait()
    first_plane = (plane + PLANES - 2 + day % 2) % PLANES
    wrapped = jnp.maximum(first_plane + NEAR - PLANES, 0)
    def serve(r, carry):
        for i in range(NEAR):
            to_plane = (first_plane + (NEAR - wrapped + i) % NEAR) % PLANES
            for k in range(WIDE):
                picked[r, i * WIDE + k] = banded[plan_ref[r, to_plane * WIDE + k]]

            def send_back(k, carry):
                wide = (band + k + 1) % WIDE
                pltpu.make_async_remote_copy(
                    src_ref=picked.at[r, i * WIDE + wide], dst_ref=returned.at[r, at],
                    send_sem=back_send, recv_sem=back_recv.at[r],
                    device_id=(to_plane * WIDE + wide, day), device_id_type=MESH,
                ).start()
                return carry

            lax.fori_loop(0, WIDE - 1, send_back, 0, unroll=True)

            @pl.when(to_plane != plane)
            def _():
                send_back(WIDE - 1, 0)

            @pl.when(to_plane == plane)
            def _():
                pltpu.make_async_copy(
                    picked.at[r, i * WIDE + band], returned.at[r, at], back_recv.at[r]
                ).start()
        return carry

    lax.fori_loop(0, ROUNDS, serve, 0)

    split(across)
    square = keep(across, square)
    wait_own(2)
    last = (beside + 2) % DAYS
    split(last)
    square = keep(last, square)
    count = float(SEG * DAYS * 2 * NFREQ)
    energy_i = jnp.sum(square, axis=1, keepdims=True) / count + EPS

    loads[2].wait()
    dot = functools.partial(jnp.dot, preferred_element_type=jnp.float32)
    bins = BIN_LO + lax.broadcasted_iota(jnp.int32, (SPB, NFREQ), 1)
    half = bins.astype(jnp.float32) * np.float32(np.pi / SEGLEN)
    half_cos, half_sin = jnp.cos(half), jnp.sin(half)
    backward = LANES - 1 - lax.broadcasted_iota(jnp.int32, (2 * SPB, LANES), 1)

    def mirrored(tile):
        return jnp.take_along_axis(tile, backward, axis=1)

    def finish(r, carry):
        pltpu.make_async_copy(returned.at[r], returned.at[r], back_recv.at[r]).wait()
        for q in range(DAYS):
            tile = returned[r, q * BANDS : (q + 1) * BANDS, : GROUPS - 1].reshape(LANES, LANES)
            tile = tile.astype(jnp.float32).T.reshape(4, 2, 2, SEG, LANES)
            for g in range(4):
                partner[:, :, q, :, g * LANES : (g + 1) * LANES] = tile[g]
        rest = jnp.concatenate(
            [
                returned[r, q * BANDS : (q + 1) * BANDS, GROUPS - 1].reshape(PIECE, LANES)
                for q in range(DAYS)
            ],
            axis=0,
        )
        rest = rest.astype(jnp.float32).T
        for q in range(DAYS):
            piece = jnp.zeros((PIECE, LANES), jnp.float32)
            for g in range(4):
                moved = rest[g * PIECE : (g + 1) * PIECE]
                if g != q:
                    moved = pltpu.roll(moved, (PIECE * (g - q)) % LANES, 1)
                piece = jnp.where(quarter == g, moved, piece)
            partner[:, :, q, :, WHOLE:] = piece.reshape(2, 2, SEG, LANES)

        def correlate(q, sums):
            sums = list(sums)
            for seg in range(SEG):
                x_re, x_im = own[0, q, seg], own[1, q, seg]
                for j in range(2):
                    y_re = partner[0, j, q, seg : seg + 1, :]
                    y_im = partner[1, j, q, seg : seg + 1, :]
                    sums[2 * j] = sums[2 * j] + x_re * y_re + x_im * y_im
                    sums[2 * j + 1] = sums[2 * j + 1] + x_im * y_re - x_re * y_im
            return tuple(sums)

        zero = jnp.zeros((SPB, NFREQ), jnp.float32)
        sums = lax.fori_loop(0, DAYS, correlate, (zero,) * 4)
        for j in range(2):
            real, imag = sums[2 * j], sums[2 * j + 1]
            cross[0, j * SPB : (j + 1) * SPB] = real * half_cos + imag * half_sin
            cross[1, j * SPB : (j + 1) * SPB] = imag * half_cos - real * half_sin
        waves = []
        for c in range(2):
            high = cross[c].astype(jnp.bfloat16)
            low = (cross[c] - high.astype(jnp.float32)).astype(jnp.bfloat16)
            both = dot(jnp.concatenate([high, low], axis=0), table[0, c])
            waves.append(both[: 2 * SPB] + both[2 * SPB :] + dot(high, table[1, c]))
        early, late = waves[0] + waves[1], waves[0] - waves[1]
        raw = jnp.concatenate(
            [mirrored(early[:, LANES:]), mirrored(early[:, :LANES]), late], axis=1
        )
        for j in range(2):
            square = jnp.zeros((SEG, LANES), jnp.float32)
            for c in range(2):
                for q in range(DAYS):
                    for t in range(TILES):
                        y = partner[c, j, q, :, t * LANES : (t + 1) * LANES]
                        square = square + y * y
            energy_j = jnp.sum(square, axis=1, keepdims=True)
            energy_j = jnp.sum(energy_j, axis=0, keepdims=True) / count + EPS
            scale = 1.0 / (jnp.sqrt(energy_j * energy_i) * np.float32(np.sqrt(count)))
            out_ref[r, j] = (raw[j * SPB : (j + 1) * SPB] * scale).astype(jnp.bfloat16)
        return carry

    lax.fori_loop(0, ROUNDS, finish, 0)

    tiles = DAYS * BANDS
    pltpu.make_async_copy(sent, sent, first_send).wait()
    rest_sent = sent.at[pl.ds(0, tiles - 1)]
    pltpu.make_async_copy(rest_sent, rest_sent, first_send).wait()

    @pl.when(jnp.logical_not(keeps_own))
    def _():
        pltpu.make_async_copy(sent.at[0], sent.at[0], first_send).wait()

    for r in range(ROUNDS):
        rest_sent = picked.at[r, pl.ds(0, NEAR * WIDE - 1)]
        pltpu.make_async_copy(rest_sent, rest_sent, back_send).wait()
    rest_sent = spectra.at[pl.ds(0, DAYS - 1)]
    pltpu.make_async_copy(rest_sent, rest_sent, own_send).wait()


def per_device(spectra, pairing, station_slot):
    x = spectra.reshape(SPB * SEG, 2, NFREQ)
    wide = jnp.pad(pairing, ((0, 0), (0, station_slot.size - BLOCKS)))
    plan = jnp.concatenate([wide, station_slot[None]], axis=0)
    hbm = pl.BlockSpec(memory_space=pltpu.HBM)
    dma = pltpu.SemaphoreType.DMA
    f32, bf16 = jnp.float32, jnp.bfloat16
    return pl.pallas_call(
        kernel,
        out_shape=jax.ShapeDtypeStruct((ROUNDS, 2, SPB, LAGS), bf16),
        in_specs=[hbm] * 3,
        out_specs=pl.BlockSpec(memory_space=pltpu.VMEM),
        scratch_shapes=[
            pltpu.VMEM((DAYS,) + x.shape, bf16),
            pltpu.SMEM(plan.shape, jnp.int32),
            pltpu.VMEM((2, SPB, SEG, NFREQ), f32),
            pltpu.VMEM((2, DAYS, SEG, SPB, NFREQ), f32),
            pltpu.VMEM((DAYS * BANDS, GROUPS, ROWS, LANES), bf16),
            pltpu.VMEM((BLOCKS, GROUPS, ROWS, LANES), bf16),
            pltpu.VMEM((ROUNDS, NEAR * WIDE, GROUPS, ROWS, LANES), bf16),
            pltpu.VMEM((ROUNDS, DAYS * BANDS, GROUPS, ROWS, LANES), bf16),
            pltpu.VMEM((2, 2, DAYS, SEG, NFREQ), f32),
            pltpu.VMEM((2, 2 * SPB, NFREQ), f32),
            pltpu.VMEM((2, 2, NFREQ, LAGS // 2), bf16),
            dma((3,)), dma, dma, dma, dma((ROUNDS,)), dma, dma((DAYS - 1,)),
        ],
        compiler_params=pltpu.CompilerParams(
            collective_id=0, has_side_effects=True, vmem_limit_bytes=55168 * 1024
        ),
        name="correlate",
    )(x, plan, jnp.asarray(lag_table()))


def solution(mesh):
    in_specs = (P("sta", "day", None, None), P(), P())
    out_specs = P(None, "day", "sta", None)
    return jax.shard_map(
        per_device, mesh=mesh, in_specs=in_specs, out_specs=out_specs, check_vma=False
    )
```

```python
import functools

import jax
import jax.numpy as jnp
import ml_dtypes
import numpy as np
from jax import lax
from jax.experimental import pallas as pl
from jax.experimental.pallas import tpu as pltpu
from jax.sharding import PartitionSpec as P

BIN_LO = 60
SEGLEN = 6000
LAGS = 512
ROUNDS = 3
EPS = 1e-06
NFREQ = 640
SPB = 8
SEG = 8
DAYS = 4
BLOCKS = 64
PLANES = 8
WIDE = 8
BANDS = 8
GROUPS = 5
ROWS = 4
HALVES = 2
NEAR = 4
LANES = 128
PIECE = 32
TILES = NFREQ // LANES
WHOLE = 512
MESH = pl.DeviceIdType.MESH
ORDER = sorted(
    ((r, i) for r in range(ROUNDS) for i in range(NEAR)), key=lambda at: (at[0], at[1])
)


def lag_table():
    bins = BIN_LO + np.arange(NFREQ, dtype=np.int64)
    halves = 2 * np.arange(LAGS // 2, dtype=np.int64) + 1
    turns = np.mod(bins[:, None] * halves[None, :], 2 * SEGLEN)
    angle = np.pi / SEGLEN * turns
    table = np.stack([np.cos(angle), np.sin(angle)]).astype(np.float32)
    high = table.astype(ml_dtypes.bfloat16)
    low = (table - high.astype(np.float32)).astype(ml_dtypes.bfloat16)
    return np.stack([high, low])


def outward(k, half):
    return half + (k + 1) // 2 * (1 - 2 * (k % 2))


def far_first(sta, k):
    plane = (sta // WIDE + outward(k // WIDE, PLANES // 2)) % PLANES
    return plane * WIDE + (sta % WIDE + k % WIDE + 1) % WIDE


def kernel(
    x_hbm, plan_hbm, table_hbm, out_ref,
    spectra, plan_ref, natural, own, sent, banded, picked, returned, partner, cross, table,
    load_sem, first_send, first_recv, back_send, back_recv, own_send, own_recv,
):
    sta, day = lax.axis_index("sta"), lax.axis_index("day")
    plane, band = sta // WIDE, sta % WIDE
    origin = (plane + band) % DAYS
    keeps_own = origin == day

    barrier = pltpu.get_barrier_semaphore()

    def greet(place, to_day):
        pl.semaphore_signal(barrier, inc=1, device_id=(place, to_day), device_id_type=MESH)

    def greet_block(k, carry):
        greet(far_first(sta, k), origin)
        return carry

    lax.fori_loop(0, BLOCKS - 1, greet_block, 0, unroll=7)

    @pl.when(jnp.logical_not(keeps_own))
    def _():
        greet(sta, origin)

    for k in range(1, DAYS):
        greet(sta, (day + k) % DAYS)

    loads = [
        pltpu.make_async_copy(source, target, load_sem.at[i])
        for i, (source, target) in enumerate(
            [(x_hbm, spectra.at[day]), (plan_hbm, plan_ref), (table_hbm, table)]
        )
    ]
    for load in loads:
        load.start()

    for load in loads[:2]:
        load.wait()

    def split(day_from):
        for c in range(2):
            part = spectra[day_from, :, c, :].astype(jnp.float32)
            natural[c] = part.reshape(SPB, SEG, NFREQ)

    split(day)
    slots = [plan_ref[ROUNDS, sta * SPB + i] for i in range(SPB)]
    order = []
    for j in range(SPB):
        at = jnp.int32(0)
        for i in range(1, SPB):
            at = jnp.where(slots[i] == j, i, at)
        order.append(at)
    pairs = [
        jnp.concatenate(
            [natural[c, order[2 * to + j]] for c in range(2) for j in range(2)], axis=0
        )
        for to in range(DAYS)
    ]
    quarter = lax.broadcasted_iota(jnp.int32, (PIECE, LANES), 1) // PIECE
    for to in range(DAYS):
        tile = jnp.concatenate(
            [pairs[to][:, g * LANES : (g + 1) * LANES] for g in range(4)], axis=0
        )
        tile = tile.T.astype(jnp.bfloat16).reshape(BANDS, GROUPS - 1, ROWS, LANES)
        sent[to * BANDS : (to + 1) * BANDS, : GROUPS - 1] = tile
    rest = []
    for g in range(4):
        piece = jnp.zeros((PIECE, LANES), jnp.float32)
        for to in range(DAYS):
            moved = pairs[to][:, WHOLE:]
            if to != g:
                moved = pltpu.roll(moved, (PIECE * (to - g)) % LANES, 1)
            piece = jnp.where(quarter == to, moved, piece)
        rest.append(piece)
    rest = jnp.concatenate(rest, axis=0).T.astype(jnp.bfloat16)
    for to in range(DAYS):
        tile = rest[to * PIECE : (to + 1) * PIECE].reshape(BANDS, ROWS, LANES)
        sent[to * BANDS : (to + 1) * BANDS, GROUPS - 1] = tile

    greetings = BLOCKS + DAYS - 1 - jnp.where(keeps_own, 1, 0)
    pl.semaphore_wait(barrier, greetings)

    beside = day + 1 - 2 * (day % 2)
    across = (day + 2) % DAYS

    def send_own(from_day, to_day, i, part=slice(None)):
        pltpu.make_async_remote_copy(
            src_ref=spectra.at[from_day, part], dst_ref=spectra.at[from_day, part], send_sem=own_send, recv_sem=own_recv.at[i],
            device_id=(sta, to_day), device_id_type=MESH,
        ).start()

    def wait_own(i):
        pltpu.make_async_copy(spectra.at[0], spectra.at[0], own_recv.at[i]).wait()

    def keep(from_day, square):
        for c in range(2):
            for seg in range(SEG):
                x = natural[c, :, seg, :]
                own[c, from_day, seg] = x
                for t in range(TILES):
                    x_t = x[:, t * LANES : (t + 1) * LANES]
                    square = square + x_t * x_t
        return square

    send_own(day, beside, 1)

    def send_first(k, carry):
        i_plane = k // WIDE
        to_plane = (plane + PLANES + (i_plane // 2 + 1) * (1 - 2 * (i_plane % 2)) + i_plane // 7 * 4) % PLANES
        turn = (k + band) % WIDE
        to_band = (day + PLANES - to_plane) % DAYS + turn % HALVES * DAYS
        to = turn // HALVES
        place = to_plane * WIDE + to_band

        @pl.when(jnp.logical_or(place != sta, to != day))
        def _():
            pltpu.make_async_remote_copy(
                src_ref=sent.at[to * BANDS + to_band], dst_ref=banded.at[sta],
                send_sem=first_send, recv_sem=first_recv, device_id=(place, to), device_id_type=MESH,
            ).start()

        return carry

    for i in range(PLANES):
        lax.fori_loop(i * WIDE, (i + 1) * WIDE, send_first, 0, unroll=True)
        send_own(day, across, 0, pl.ds(i * SPB, SPB))

    @pl.when(keeps_own)
    def _():
        pltpu.make_async_copy(sent.at[day * BANDS + band], banded.at[sta], first_recv).start()

    square = keep(day, jnp.zeros((SPB, LANES), jnp.float32))
    wait_own(1)
    split(beside)
    square = keep(beside, square)
    wait_own(0)
    send_own(across, beside, 2)

    at = origin * BANDS + band
    pltpu.make_async_copy(banded, banded, first_recv).wait()
    first_plane = (plane + PLANES - 2 + day % 2) % PLANES
    wrapped = jnp.maximum(first_plane + NEAR - PLANES, 0)
    for r, i in ORDER:
        to_plane = (first_plane + (NEAR - wrapped + i) % NEAR) % PLANES
        for k in range(WIDE):
            picked[r, i * WIDE + k] = banded[plan_ref[r, to_plane * WIDE + k]]

        def send_back(k, carry):
            wide = (band + k + 1) % WIDE
            pltpu.make_async_remote_copy(
                src_ref=picked.at[r, i * WIDE + wide], dst_ref=returned.at[r, at],
                send_sem=back_send, recv_sem=back_recv.at[r],
                device_id=(to_plane * WIDE + wide, day), device_id_type=MESH,
            ).start()
            return carry

        lax.fori_loop(0, WIDE - 1, send_back, 0, unroll=True)

        @pl.when(to_plane != plane)
        def _():
            send_back(WIDE - 1, 0)

        @pl.when(to_plane == plane)
        def _():
            pltpu.make_async_copy(
                picked.at[r, i * WIDE + band], returned.at[r, at], back_recv.at[r]
            ).start()

    split(across)
    square = keep(across, square)
    wait_own(2)
    last = (beside + 2) % DAYS
    split(last)
    square = keep(last, square)
    count = float(SEG * DAYS * 2 * NFREQ)
    energy_i = jnp.sum(square, axis=1, keepdims=True) / count + EPS

    loads[2].wait()
    dot = functools.partial(jnp.dot, preferred_element_type=jnp.float32)
    bins = BIN_LO + lax.broadcasted_iota(jnp.int32, (SPB, NFREQ), 1)
    half = bins.astype(jnp.float32) * np.float32(np.pi / SEGLEN)
    half_cos, half_sin = jnp.cos(half), jnp.sin(half)
    backward = LANES - 1 - lax.broadcasted_iota(jnp.int32, (2 * SPB, LANES), 1)

    def mirrored(tile):
        return jnp.take_along_axis(tile, backward, axis=1)

    for r in range(ROUNDS):
        pltpu.make_async_copy(returned.at[r], returned.at[r], back_recv.at[r]).wait()
        for q in range(DAYS):
            tile = returned[r, q * BANDS : (q + 1) * BANDS, : GROUPS - 1].reshape(LANES, LANES)
            tile = tile.astype(jnp.float32).T.reshape(4, 2, 2, SEG, LANES)
            for g in range(4):
                partner[:, :, q, :, g * LANES : (g + 1) * LANES] = tile[g]
        rest = jnp.concatenate(
            [
                returned[r, q * BANDS : (q + 1) * BANDS, GROUPS - 1].reshape(PIECE, LANES)
                for q in range(DAYS)
            ],
            axis=0,
        )
        rest = rest.astype(jnp.float32).T
        for q in range(DAYS):
            piece = jnp.zeros((PIECE, LANES), jnp.float32)
            for g in range(4):
                moved = rest[g * PIECE : (g + 1) * PIECE]
                if g != q:
                    moved = pltpu.roll(moved, (PIECE * (g - q)) % LANES, 1)
                piece = jnp.where(quarter == g, moved, piece)
            partner[:, :, q, :, WHOLE:] = piece.reshape(2, 2, SEG, LANES)

        def correlate(q, sums):
            sums = list(sums)
            for seg in range(SEG):
                x_re, x_im = own[0, q, seg], own[1, q, seg]
                for j in range(2):
                    y_re = partner[0, j, q, seg : seg + 1, :]
                    y_im = partner[1, j, q, seg : seg + 1, :]
                    sums[2 * j] = sums[2 * j] + x_re * y_re + x_im * y_im
                    sums[2 * j + 1] = sums[2 * j + 1] + x_im * y_re - x_re * y_im
            return tuple(sums)

        zero = jnp.zeros((SPB, NFREQ), jnp.float32)
        sums = lax.fori_loop(0, DAYS, correlate, (zero,) * 4)
        for j in range(2):
            real, imag = sums[2 * j], sums[2 * j + 1]
            cross[0, j * SPB : (j + 1) * SPB] = real * half_cos + imag * half_sin
            cross[1, j * SPB : (j + 1) * SPB] = imag * half_cos - real * half_sin
        waves = []
        for c in range(2):
            high = cross[c].astype(jnp.bfloat16)
            low = (cross[c] - high.astype(jnp.float32)).astype(jnp.bfloat16)
            both = dot(jnp.concatenate([high, low], axis=0), table[0, c])
            waves.append(both[: 2 * SPB] + both[2 * SPB :] + dot(high, table[1, c]))
        early, late = waves[0] + waves[1], waves[0] - waves[1]
        raw = jnp.concatenate(
            [mirrored(early[:, LANES:]), mirrored(early[:, :LANES]), late], axis=1
        )
        for j in range(2):
            square = jnp.zeros((SEG, LANES), jnp.float32)
            for c in range(2):
                for q in range(DAYS):
                    for t in range(TILES):
                        y = partner[c, j, q, :, t * LANES : (t + 1) * LANES]
                        square = square + y * y
            energy_j = jnp.sum(square, axis=1, keepdims=True)
            energy_j = jnp.sum(energy_j, axis=0, keepdims=True) / count + EPS
            scale = 1.0 / (jnp.sqrt(energy_j * energy_i) * np.float32(np.sqrt(count)))
            out_ref[r, j] = (raw[j * SPB : (j + 1) * SPB] * scale).astype(jnp.bfloat16)

    tiles = DAYS * BANDS
    pltpu.make_async_copy(sent, sent, first_send).wait()
    rest_sent = sent.at[pl.ds(0, tiles - 1)]
    pltpu.make_async_copy(rest_sent, rest_sent, first_send).wait()

    @pl.when(jnp.logical_not(keeps_own))
    def _():
        pltpu.make_async_copy(sent.at[0], sent.at[0], first_send).wait()

    for r in range(ROUNDS):
        rest_sent = picked.at[r, pl.ds(0, NEAR * WIDE - 1)]
        pltpu.make_async_copy(rest_sent, rest_sent, back_send).wait()
    rest_sent = spectra.at[pl.ds(0, DAYS - 1)]
    pltpu.make_async_copy(rest_sent, rest_sent, own_send).wait()


def per_device(spectra, pairing, station_slot):
    x = spectra.reshape(SPB * SEG, 2, NFREQ)
    wide = jnp.pad(pairing, ((0, 0), (0, station_slot.size - BLOCKS)))
    plan = jnp.concatenate([wide, station_slot[None]], axis=0)
    hbm = pl.BlockSpec(memory_space=pltpu.HBM)
    dma = pltpu.SemaphoreType.DMA
    f32, bf16 = jnp.float32, jnp.bfloat16
    return pl.pallas_call(
        kernel,
        out_shape=jax.ShapeDtypeStruct((ROUNDS, 2, SPB, LAGS), bf16),
        in_specs=[hbm] * 3,
        out_specs=pl.BlockSpec(memory_space=pltpu.VMEM),
        scratch_shapes=[
            pltpu.VMEM((DAYS,) + x.shape, bf16),
            pltpu.SMEM(plan.shape, jnp.int32),
            pltpu.VMEM((2, SPB, SEG, NFREQ), f32),
            pltpu.VMEM((2, DAYS, SEG, SPB, NFREQ), f32),
            pltpu.VMEM((DAYS * BANDS, GROUPS, ROWS, LANES), bf16),
            pltpu.VMEM((BLOCKS, GROUPS, ROWS, LANES), bf16),
            pltpu.VMEM((ROUNDS, NEAR * WIDE, GROUPS, ROWS, LANES), bf16),
            pltpu.VMEM((ROUNDS, DAYS * BANDS, GROUPS, ROWS, LANES), bf16),
            pltpu.VMEM((2, 2, DAYS, SEG, NFREQ), f32),
            pltpu.VMEM((2, 2 * SPB, NFREQ), f32),
            pltpu.VMEM((2, 2, NFREQ, LAGS // 2), bf16),
            dma((3,)), dma, dma, dma, dma((ROUNDS,)), dma, dma((DAYS - 1,)),
        ],
        compiler_params=pltpu.CompilerParams(
            collective_id=0, has_side_effects=True, vmem_limit_bytes=55168 * 1024
        ),
        name="correlate",
    )(x, plan, jnp.asarray(lag_table()))


def solution(mesh):
    in_specs = (P("sta", "day", None, None), P(), P())
    out_specs = P(None, "day", "sta", None)
    return jax.shard_map(
        per_device, mesh=mesh, in_specs=in_specs, out_specs=out_specs, check_vma=False
    )
```
